512 devices in a mesh: shot: 32 (over y, x), px: 4 (over z_lo, core), py: 4 (over z_hi).
Axes of the slice: x: 4, y: 8, z: 8 (z_hi: 4, z_lo: 2; z = z_hi * 2 + z_lo), core: 2. Of those that a mesh axis runs over, the one named last changes fastest.
Arguments:
- fwd_now: float32 [32, 128, 64, 256], P('shot', 'px', 'py'), may hold values from -6 to 6
- fwd_next: float32 [32, 128, 64, 256], P('shot', 'px', 'py'), may hold values from -6 to 6
- adj_now: float32 [32, 128, 64, 256], P('shot', 'px', 'py'), may hold values from -6 to 6
- adj_next: float32 [32, 128, 64, 256], P('shot', 'px', 'py'), may hold values from -6 to 6
- velocity: float32 [128, 128, 1024], P('shot', 'px', 'py'), may hold values from 1.5 to 4.5
- density: float32 [128, 128, 1024], P('shot', 'px', 'py'), may hold values from 1 to 2.6
- gradient_in: float32 [128, 128, 1024], P('shot', 'px', 'py'), may hold values from -6 to 6
- block_home: int32 [8, 16], replicated, may hold values from 0 to 127, as said below
- aperture_col: int32 [32], P('shot'), may hold values from 0 to 7
- source_cell: int32 [32], P('shot'), may hold values from 0 to 2097151
- source_amp: float32 [32], P('shot'), may hold values from -6 to 6
- receiver_cell: int32 [32, 256], P('shot'), may hold values from 0 to 2097151
- receiver_residual: float32 [32, 256], P('shot'), may hold values from -6 to 6
Outputs:
- fwd_prev: float32 [32, 128, 64, 256], P('shot', 'px', 'py')
- adj_prev: float32 [32, 128, 64, 256], P('shot', 'px', 'py')
- gradient: float32 [128, 128, 1024], P('shot', 'px', 'py')
The draws below stay inside these ranges and needn't reach their ends.
Inputs may be any that keep to these rules, and one draw needn't show every extreme that they name: `block_home`: each of the 8 columns has its 16 depth blocks on 16 different owners, the owner of block b being b // 4; every model block index appears exactly once.
All inputs are finite; a program needn't handle non-finite values.
Results may differ from the reference program's by a relative error of at most 0.000092.
Values sent between devices are 32-bit elements; how exact they have to be, the bound alone decides.
A program may use at most 64 MiB of HBM per device.

```python
import math
import jax
import jax.numpy as jnp
import numpy as np
from jax import lax

BZ = 16
BLK_DEV = 4
NREC = 256
ZB = 16
NZ = 256
NXA = 128
NYA = 64
COLS = 8
SLOTS = 128
N_SHOT = 32


def draw_block_home(key, part):
    key = jax.random.fold_in(key, 11)
    key_owner, key_shift, key_within = jax.random.split(key, 3)
    owner_order = jax.random.permutation(key_owner, N_SHOT).astype(jnp.int32)
    shifts = jax.random.randint(key_shift, (BLK_DEV,), 0, N_SHOT // 2).astype(jnp.int32)
    within_order = jax.random.permutation(key_within, BLK_DEV).astype(jnp.int32)
    column = jnp.arange(COLS, dtype=jnp.int32)[:, None]
    depth_block = jnp.arange(ZB, dtype=jnp.int32)[None, :]
    raw_owner = (2 * depth_block + column % 2 + 2 * shifts[column // 2]) % N_SHOT
    owner = owner_order[raw_owner]
    within = within_order[column // 2]
    return (owner * BLK_DEV + within).astype(jnp.int32)


def touch_ends(array, rng, low, high):
    longest = array.shape.index(max(array.shape))
    spots = []
    for shift in (0, 1):
        where = [jax.random.randint(jax.random.fold_in(rng, axis), (), 0, length) for axis, length in enumerate(array.shape)]
        where[longest] = (where[longest] + shift) % array.shape[longest]
        spots.append(tuple(where))
    return array.at[spots[0]].set(low).at[spots[1]].set(high)


def level_of(rng, dims, cuts, low, largest):
    gain, own = 1.0, jax.random.fold_in(rng, 6)
    for position, blocks in cuts:
        steps = jnp.exp(jax.random.uniform(jax.random.fold_in(own, position), (blocks,), jnp.float32, low / len(cuts), largest / len(cuts)))
        gain = gain * jnp.repeat(steps, dims[position] // blocks).reshape([-1 if axis == position else 1 for axis in range(len(dims))])
    return gain


def cumulative_ranks(count, slope):
    portions = [(1 << 20) // math.isqrt(grade ** slope) + 1 for grade in range(1, count + 1)]
    scale = 1 + sum(portions) // (1 << 30)
    return np.cumsum(np.array([max(1, weight // scale) for weight in portions]))


def ranked(rng, extent, count, lean):
    listing = cumulative_ranks(count, lean)
    pick = jax.random.randint(jax.random.fold_in(rng, 1), extent, 0, int(listing[count - 1]))
    rank = jnp.searchsorted(jnp.asarray(listing, jnp.int32), pick, side="right")
    return jax.random.permutation(jax.random.fold_in(rng, 2), count)[rank].astype(jnp.int32)


def scatter_about(own_key, shape, spread, most, cuts=(), kind=jnp.bfloat16):
    result = jax.random.normal(own_key, shape, jnp.float32) * spread
    if len(cuts) > 0:
        result = level_of(own_key, shape, cuts, -0.22, 0.18) * result
    return jnp.clip(result, min=-most, max=most).astype(kind)


def setup_inputs(seed: int = 0) -> dict:
    arg_keys = jax.random.split(jax.random.key(seed), 14)
    fwd_now = scatter_about(arg_keys[0], (N_SHOT, NXA, NYA, NZ), 1.0, 6.0, ((0, 32), (1, 4), (2, 4)), jnp.float32)
    fwd_next = scatter_about(arg_keys[1], (N_SHOT, NXA, NYA, NZ), 1.0, 6.0, ((0, 32), (1, 4), (2, 4)), jnp.float32)
    adj_now = scatter_about(arg_keys[2], (N_SHOT, NXA, NYA, NZ), 1.0, 6.0, ((0, 32), (1, 4), (2, 4)), jnp.float32)
    adj_next = scatter_about(arg_keys[3], (N_SHOT, NXA, NYA, NZ), 1.0, 6.0, ((0, 32), (1, 4), (2, 4)), jnp.float32)
    velocity = jnp.clip(1.5 + 3.0 * jax.random.uniform(arg_keys[4], (SLOTS, NXA, NYA * BZ), jnp.float32) ** level_of(arg_keys[4], (SLOTS, NXA, NYA * BZ), ((0, 32), (1, 4), (2, 4)), -0.2, 0.2), 1.5, 4.5)
    density = jnp.clip(1.0 + 1.5999999 * jax.random.uniform(arg_keys[5], (SLOTS, NXA, NYA * BZ), jnp.float32) ** level_of(arg_keys[5], (SLOTS, NXA, NYA * BZ), ((0, 32), (1, 4), (2, 4)), -0.2, 0.2), 1.0, 2.6)
    gradient_in = scatter_about(arg_keys[6], (SLOTS, NXA, NYA * BZ), 1.0, 6.0, ((0, 32), (1, 4), (2, 4)), jnp.float32)
    block_home = draw_block_home(jax.random.fold_in(arg_keys[13], 71), 0)
    aperture_col = touch_ends(ranked(arg_keys[8], (N_SHOT,), COLS, 2), jax.random.fold_in(arg_keys[8], 3), 0, COLS - 1).astype(jnp.int32)
    source_cell = touch_ends(jax.random.randint(arg_keys[9], (N_SHOT,), 0, NXA * NYA * NZ), jax.random.fold_in(arg_keys[9], 1), 0, (NXA * NYA * NZ) - 1).astype(jnp.int32)
    source_amp = scatter_about(arg_keys[10], (N_SHOT,), 1.0, 6.0, ((0, 32),), jnp.float32)
    receiver_cell = touch_ends(jax.random.randint(arg_keys[11], (N_SHOT, NREC), 0, NXA * NYA * NZ), jax.random.fold_in(arg_keys[11], 1), 0, (NXA * NYA * NZ) - 1).astype(jnp.int32)
    receiver_residual = scatter_about(arg_keys[12], (N_SHOT, NREC), 1.0, 6.0, ((0, 32),), jnp.float32)
    return {"fwd_now": fwd_now, "fwd_next": fwd_next, "adj_now": adj_now, "adj_next": adj_next, "velocity": velocity, "density": density, "gradient_in": gradient_in, "block_home": block_home, "aperture_col": aperture_col, "source_cell": source_cell, "source_amp": source_amp, "receiver_cell": receiver_cell, "receiver_residual": receiver_residual}


COEFS = (1225.0 / 1024.0, -245.0 / 3072.0, 49.0 / 5120.0, -5.0 / 7168.0)
COURANT2 = 0.01


def cut(values, begin, length, along):
    return lax.slice_in_dim(values, begin, begin + length, axis=along)


def forward_diff(extended, offset, first_face, face_count, along):
    summed = None
    for reach, weight in enumerate(COEFS, 1):
        term = weight * (cut(extended, first_face + reach + offset, face_count, along) - cut(extended, first_face + 1 - reach + offset, face_count, along))
        summed = term if summed is None else summed + term
    return summed


def backward_diff(extended, offset, cell_count, along):
    summed = None
    for reach, weight in enumerate(COEFS, 1):
        term = weight * (cut(extended, reach - 1 + offset, cell_count, along) - cut(extended, offset - reach, cell_count, along))
        summed = term if summed is None else summed + term
    return summed


def face_flux(forward, rho_low, rho_high, face_index, total_cells, along_three):
    mask_shape = [1, 1, 1]
    mask_shape[along_three] = face_index.shape[0]
    inside = ((face_index >= 0) & (face_index <= total_cells - 2)).reshape(mask_shape)
    safe = jnp.where(inside, rho_low + rho_high, 1.0)
    return jnp.where(inside, 2.0 * forward / safe, 0.0)


def divergence(fields, density):
    summed = None
    for along in (1, 2, 3):
        cells = fields.shape[along]
        padding = [(0, 0)] * 4
        padding[along] = (3, 4)
        forward = forward_diff(jnp.pad(fields, padding), 3, 0, cells, along)
        rho_pad = [(0, 0)] * 3
        rho_pad[along - 1] = (0, 1)
        rho_ext = jnp.pad(density, rho_pad)
        flux = face_flux(forward, cut(rho_ext, 0, cells, along - 1), cut(rho_ext, 1, cells, along - 1), jnp.arange(cells, dtype=jnp.int32), cells, along - 1)
        flux_pad = [(0, 0)] * 4
        flux_pad[along] = (4, 3)
        term = backward_diff(jnp.pad(flux, flux_pad), 4, cells, along)
        summed = term if summed is None else summed + term
    return summed


def reference(fwd_now, fwd_next, adj_now, adj_next, velocity, density, gradient_in, block_home, aperture_col, source_cell, source_amp, receiver_cell, receiver_residual):
    def pencil(store, slots):
        picked = store[slots].reshape(ZB, NXA, NYA, BZ)
        return picked.transpose(1, 2, 0, 3).reshape(NXA, NYA, NZ)

    def per_group(group):
        slots = block_home[aperture_col[group]]
        vel = pencil(velocity, slots)
        dens = pencil(density, slots)
        fields = jnp.stack([fwd_now[group], adj_now[group]])
        lap = divergence(fields, dens)
        update = (COURANT2 * (dens * vel * vel)) * lap
        fwd_new = 2.0 * fwd_now[group] - fwd_next[group] + update[0]
        adj_new = 2.0 * adj_now[group] - adj_next[group] + update[1]
        fwd_new = fwd_new.reshape(-1).at[source_cell[group]].add(-source_amp[group]).reshape(NXA, NYA, NZ)
        adj_new = adj_new.reshape(-1).at[receiver_cell[group]].add(receiver_residual[group]).reshape(NXA, NYA, NZ)
        contribution = (2.0 / vel) * adj_now[group] * (fwd_next[group] - 2.0 * fwd_now[group] + fwd_new)
        slabs = contribution.reshape(NXA, NYA, ZB, BZ).transpose(2, 0, 1, 3).reshape(ZB, NXA, NYA * BZ)
        return fwd_new, adj_new, slabs

    fwd_prev, adj_prev, slabs = lax.map(per_group, jnp.arange(N_SHOT, dtype=jnp.int32))
    all_slots = block_home[aperture_col].reshape(-1)
    gradient = gradient_in.at[all_slots].add(slabs.reshape(N_SHOT * ZB, NXA, NYA * BZ))
    return fwd_prev, adj_prev, gradient
```

```python
import functools

import jax
import jax.numpy as jnp
from jax import lax
from jax.experimental import pallas as pl
from jax.experimental.pallas import tpu as pltpu
from jax.sharding import PartitionSpec as P

COEFS = (1225.0 / 1024.0, -245.0 / 3072.0, 49.0 / 5120.0, -5.0 / 7168.0)
COURANT2 = 0.01
MESH = pl.DeviceIdType.MESH
HIGHEST = lax.Precision.HIGHEST

LX, LY, LZ = 32, 16, 256
NY, NX = 8, 4
NPX, NPY = 4, 4
BLOCKS, HELD, BZ = 16, 4, 16
H = 8


def dot(a, b):
    return jnp.dot(a, b, precision=HIGHEST, preferred_element_type=jnp.float32)


def band(delta, pairs):
    total = jnp.zeros(delta.shape, jnp.float32)
    for offset, weight in pairs:
        total = jnp.where(delta == offset, jnp.float32(weight), total)
    return total


FORWARD = tuple((r, c) for r, c in enumerate(COEFS, 1)) + tuple((1 - r, -c) for r, c in enumerate(COEFS, 1))
BACKWARD = tuple((r - 1, c) for r, c in enumerate(COEFS, 1)) + tuple((-r, -c) for r, c in enumerate(COEFS, 1))


def swap_groups(tiles):
    lane = lax.broadcasted_iota(jnp.int32, (8, 128), 1)
    tiles = [list(t) for t in tiles]
    for a in range(8):
        tiles[a][1], tiles[a + 8][0] = tiles[a + 8][0], tiles[a][1]
    for k in (4, 2, 1):
        set_bit = ((lane >> 4) & k) != 0
        for a in range(16):
            if a & k:
                continue
            for half in range(2):
                low, high = tiles[a][half], tiles[a + k][half]
                tiles[a][half] = jnp.where(set_bit, pltpu.roll(high, 16 * k, 1), low)
                tiles[a + k][half] = jnp.where(set_bit, high, pltpu.roll(low, 128 - 16 * k, 1))
    return tiles


def kernel(
    fwd_now, adj_now, fwd_next, adj_next, velocity, density, gradient_in,
    home_v, home_s, col_s, src_cell, src_amp, rec_cell, rec_val,
    fwd_out, adj_out, grad_out,
    u, nx, fx, fy, fz, lap, rho, vel,
    bd0, bd1, bd2, bd3, bd4, bd5, bd6, bd7,
    bv0, bv1, bv2, bv3, bv4, bv5, bv6, bv7,
    std, stv, gotd, gotv, tmp, sy, hy,
    contrib, gst, grecv,
    p0, p1, p2, p3, p4, p5, p6, p7, rs,
    dz, dzb, my, myb,
    tbl_v, tbl_s, colbuf, colrecv, cols_s,
    loc_sem, agd_s, agd_r, agv_s, agv_r, xd_s, xd_r, xv_s, xv_r, xg_s, xg_r,
    rs_s, rs_r, uh_s, uh_r, dh_s, dh_r, col_ss, col_rs, out_sem,
):
    bd = (bd0, bd1, bd2, bd3, bd4, bd5, bd6, bd7)
    bv = (bv0, bv1, bv2, bv3, bv4, bv5, bv6, bv7)
    part = (p0, p1, p2, p3, p4, p5, p6, p7)
    shot = lax.axis_index("shot")
    px = lax.axis_index("px")
    py = lax.axis_index("py")
    gx = lax.rem(shot, NX)
    gy = shot // NX

    def along_x(e):
        return {"shot": gy * NX + lax.rem(gx + e, NX)}

    def along_y(e):
        return {"shot": lax.rem(gy + e, NY) * NX + gx}

    loads = [
        pltpu.make_async_copy(density, bd0, loc_sem.at[0]),
        pltpu.make_async_copy(fwd_now, u.at[0, pl.ds(H, LX), pl.ds(H, LY), :], loc_sem.at[1]),
        pltpu.make_async_copy(adj_now, u.at[1, pl.ds(H, LX), pl.ds(H, LY), :], loc_sem.at[2]),
        pltpu.make_async_copy(fwd_next, nx.at[0], loc_sem.at[3]),
        pltpu.make_async_copy(adj_next, nx.at[1], loc_sem.at[4]),
        pltpu.make_async_copy(velocity, bv0, loc_sem.at[5]),
        pltpu.make_async_copy(gradient_in, rs.at[8], loc_sem.at[6]),
    ]
    for c in loads:
        c.start()

    def fill(i, _):
        rho[i] = jnp.ones((LY + 2 * H, LZ), jnp.float32)
        return 0

    lax.fori_loop(0, LX + 2 * H, fill, 0)

    def zero_rows(start):
        def body(i, _):
            u[0, H + i, start : start + H, :] = jnp.zeros((H, LZ), jnp.float32)
            u[1, H + i, start : start + H, :] = jnp.zeros((H, LZ), jnp.float32)
            return 0

        lax.fori_loop(0, LX, body, 0)

    def zero_slabs(start):
        def body(i, _):
            u[0, start + i, H : H + LY, :] = jnp.zeros((LY, LZ), jnp.float32)
            u[1, start + i, H : H + LY, :] = jnp.zeros((LY, LZ), jnp.float32)
            return 0

        lax.fori_loop(0, H, body, 0)

    pl.when(py == 0)(lambda: zero_rows(0))
    pl.when(py == NPY - 1)(lambda: zero_rows(H + LY))
    pl.when(px == 0)(lambda: zero_slabs(0))
    pl.when(px == NPX - 1)(lambda: zero_slabs(H + LX))

    barrier = pltpu.get_barrier_semaphore()
    for target in [along_y(1), along_y(NY - 1)] + [along_x(e) for e in range(1, NX)]:
        pl.semaphore_signal(barrier, inc=1, device_id=target, device_id_type=MESH)
    sides = {
        "px_up": (px < NPX - 1, px > 0, {"px": px + 1}),
        "px_down": (px > 0, px < NPX - 1, {"px": px - 1}),
        "py_up": (py < NPY - 1, py > 0, {"py": py + 1}),
        "py_down": (py > 0, py < NPY - 1, {"py": py - 1}),
    }
    for has, _, target in sides.values():

        @pl.when(has)
        def _():
            pl.semaphore_signal(barrier, inc=1, device_id=target, device_id_type=MESH)

    lane8 = lax.broadcasted_iota(jnp.int32, (8, 128), 1)
    within = jnp.zeros((8, 128), jnp.int32)
    depth_of = jnp.zeros((8, 128), jnp.int32)
    for m in range(BLOCKS):
        h = home_v[:, m : m + 1]
        hit = (h >> 2) == lane8
        within = jnp.where(hit, (h & 3) + 1, within)
        depth_of = jnp.where(hit, m, depth_of)
    tbl_v[0] = within
    tbl_v[1] = depth_of
    table_copy = pltpu.make_async_copy(tbl_v, tbl_s, loc_sem.at[7])
    table_copy.start()
    my_col = col_s[0]
    colbuf[...] = jnp.zeros((8, 128), jnp.int32) + my_col

    present = [jnp.where(has, 1, 0) for has, _, _ in sides.values()]
    pl.semaphore_wait(barrier, NX + 1 + sum(present))

    def remote(src, dst, ss, rr, target):
        return pltpu.make_async_remote_copy(
            src_ref=src, dst_ref=dst, send_sem=ss, recv_sem=rr, device_id=target, device_id_type=MESH
        )

    col_copies = [
        remote(colbuf, colrecv.at[e - 1], col_ss.at[e - 1], col_rs.at[e - 1], along_x(e)) for e in range(1, NX)
    ]
    for c in col_copies:
        c.start()

    up, down = along_y(1), along_y(NY - 1)

    def gather(own, b, ss, rr):
        return {
            1: remote(own, b[1], ss.at[1], rr.at[1], up),
            7: remote(own, b[7], ss.at[7], rr.at[7], down),
            2: remote(b[1], b[2], ss.at[2], rr.at[2], up),
            6: remote(b[7], b[6], ss.at[6], rr.at[6], down),
            3: remote(b[2], b[3], ss.at[3], rr.at[3], up),
            5: remote(b[6], b[5], ss.at[5], rr.at[5], down),
            4: remote(b[3].at[pl.ds(0, 2)], b[4].at[pl.ds(0, 2)], ss.at[4], rr.at[4], up),
            0: remote(b[5].at[pl.ds(2, 2)], b[4].at[pl.ds(2, 2)], ss.at[0], rr.at[0], down),
        }

    agd = gather(density, bd, agd_s, agd_r)
    agv = gather(velocity, bv, agv_s, agv_r)
    agd[1].start()
    agd[7].start()

    def halo(f, field):
        s, r = uh_s, uh_r
        return {
            "py_up": remote(field.at[:, pl.ds(LY - H, H), :], u.at[f, pl.ds(H, LX), pl.ds(0, H), :], s.at[f, 0], r.at[f, 0], sides["py_up"][2]),
            "py_down": remote(field.at[:, pl.ds(0, H), :], u.at[f, pl.ds(H, LX), pl.ds(H + LY, H), :], s.at[f, 1], r.at[f, 1], sides["py_down"][2]),
            "px_up": remote(field.at[pl.ds(LX - H, H)], u.at[f, pl.ds(0, H), pl.ds(H, LY), :], s.at[f, 2], r.at[f, 2], sides["px_up"][2]),
            "px_down": remote(field.at[pl.ds(0, H)], u.at[f, pl.ds(H + LX, H), pl.ds(H, LY), :], s.at[f, 3], r.at[f, 3], sides["px_down"][2]),
        }

    def start_sides(copies):
        for name, c in copies.items():
            pl.when(sides[name][0])(c.start)

    def wait_sides(copies):
        for name, c in copies.items():
            pl.when(sides[name][1])(c.wait_recv)

    def finish_sides(copies):
        for name, c in copies.items():
            pl.when(sides[name][0])(c.wait_send)

    halos = [halo(0, fwd_now), halo(1, adj_now)]
    start_sides(halos[0])
    start_sides(halos[1])

    for c in col_copies:
        c.wait_recv()
    cols_copy = pltpu.make_async_copy(colrecv, cols_s, loc_sem.at[8])
    cols_copy.start()
    table_copy.wait()
    cols_copy.wait()
    cols = [my_col] + [cols_s[NX - j - 1, 0, 0] for j in range(1, NX)]

    def owner_at(d):
        return lax.rem(gy + NY - d, NY) * NX + gx

    def within_of(j, d):
        return tbl_s[0, cols[j], owner_at(d)]

    def serve(b, stage, got, ss, rr, d):
        out = []
        for e in range(1, NX):
            stage[e - 1, d] = b[d][jnp.maximum(within_of(e, d) - 1, 0)]
            c = remote(stage.at[e - 1, d], got.at[e * NY + d], ss.at[e - 1, d], rr.at[e - 1, d], along_x(e))
            c.start()
            out.append(c)
        got[d] = b[d][jnp.maximum(within_of(0, d) - 1, 0)]
        return out

    xd, xv = [], []

    def serve_d(*slots):
        for d in slots:
            xd.extend(serve(bd, std, gotd, xd_s, xd_r, d))

    def serve_v(*slots):
        for d in slots:
            xv.extend(serve(bv, stv, gotv, xv_s, xv_r, d))

    def place_of(m):
        owner = home_s[my_col, m] >> 2
        return ((gx - (owner & 3)) & 3) * NY + ((gy - (owner >> 2)) & 7)

    loads[0].wait()
    serve_d(0)

    def build(i, _):
        start = pl.multiple_of(i * 32, 32)
        row = lax.broadcasted_iota(jnp.int32, (32, 256), 0) + start
        colm = lax.broadcasted_iota(jnp.int32, (32, 256), 1)
        forward = jnp.where(colm < LZ - 1, band(row - colm, FORWARD), 0.0)
        dz[pl.ds(start, 32), :] = forward
        dzb[pl.ds(start, 32), :] = band(row - colm, BACKWARD)
        same = (row >> 5) == (colm >> 5)
        my[pl.ds(start, 32), :] = jnp.where(same, band(colm - row, FORWARD), 0.0)
        return 0

    lax.fori_loop(0, 8, build, 0)

    def build_back(i, _):
        start = pl.multiple_of(i * 32, 32)
        row = lax.broadcasted_iota(jnp.int32, (32, 256), 0) + start
        colm = lax.broadcasted_iota(jnp.int32, (32, 256), 1)
        same = (row >> 4) == (colm >> 5)
        delta = ((colm & 31) - H) - (row & 15)
        myb[pl.ds(start, 32), :] = jnp.where(same, band(delta, BACKWARD), 0.0)
        return 0

    lax.fori_loop(0, 4, build_back, 0)

    agd[1].wait_recv()
    agd[2].start()
    agd[7].wait_recv()
    agd[6].start()
    serve_d(1, 7)

    loads[1].wait()
    loads[2].wait()

    def forward_z(f):
        def body(g, _):
            block = u[f, pl.ds(H + 8 * g, 8), H : H + LY, :].reshape(8 * LY, LZ)
            fz[f, pl.ds(8 * g, 8)] = dot(block, dz[...]).reshape(8, LY, LZ)
            return 0

        lax.fori_loop(0, 4, body, 0)

    forward_z(0)
    agd[2].wait_recv()
    agd[3].start()
    agd[6].wait_recv()
    agd[5].start()
    serve_d(2, 6)
    forward_z(1)

    agd[3].wait_recv()
    agd[4].start()
    agd[5].wait_recv()
    agd[0].start()
    agv[1].start()
    agv[7].start()
    serve_d(3, 5)

    cell = rec_cell[...]
    cell_x = (cell >> 14) - px * LX
    cell_y = ((cell >> 8) & 63) - py * LY
    cell_z = cell & 255
    here = (cell_x >= 0) & (cell_x < LX) & (cell_y >= 0) & (cell_y < LY)
    spot = jnp.where(here, cell_x * LY + cell_y, -1)
    by_depth = jnp.where(lax.broadcasted_iota(jnp.int32, (LZ, 256), 0) == cell_z, rec_val[...], 0.0)
    loads[3].wait()
    loads[4].wait()

    def bases(g, _):
        start = pl.multiple_of(g * 128, 128)
        at = (lax.broadcasted_iota(jnp.int32, (128, 256), 0) + start == spot).astype(jnp.float32)
        added = lax.dot_general(
            at, by_depth, (((1,), (1,)), ((), ())), precision=HIGHEST, preferred_element_type=jnp.float32
        ).reshape(8, LY, LZ)
        rows = pl.ds(8 * g, 8)
        nx[0, rows] = 2.0 * u[0, pl.ds(H + 8 * g, 8), H : H + LY, :] - nx[0, rows]
        nx[1, rows] = 2.0 * u[1, pl.ds(H + 8 * g, 8), H : H + LY, :] - nx[1, rows] + added
        return 0

    lax.fori_loop(0, 4, bases, 0)

    agd[4].wait_recv()
    agd[0].wait_recv()
    serve_d(4)
    loads[5].wait()
    serve_v(0)

    def forward_xy(f):
        def body_x(k, _):
            total = None
            for r, weight in enumerate(COEFS, 1):
                term = weight * (u[f, k + 4 + r, H : H + LY, :] - u[f, k + 5 - r, H : H + LY, :])
                total = term if total is None else total + term
            fx[f, k] = total
            return 0

        lax.fori_loop(0, LX + 7, body_x, 0)

        def body_y(g, _):
            block = u[f, pl.ds(H + 8 * g, 8)].reshape(8 * (LY + 2 * H), LZ)
            fy[f, pl.ds(8 * g, 8)] = dot(my[...], block).reshape(8, LY + 2 * H, LZ)
            return 0

        lax.fori_loop(0, 4, body_y, 0)

    wait_sides(halos[0])
    forward_xy(0)

    agv[1].wait_recv()
    agv[2].start()
    agv[7].wait_recv()
    agv[6].start()
    serve_v(1, 7)

    def to_pencil(got, store):
        places = [place_of(m) for m in range(BLOCKS)]

        def body(g, _):
            tiles = []
            for m in range(BLOCKS):
                slab = got[places[m], pl.ds(pl.multiple_of(8 * g, 8), 8), :]
                tiles.append([slab[:, :128], slab[:, 128:]])
            tiles = swap_groups(tiles)
            for y in range(LY):
                for half in range(2):
                    tmp[half, pl.ds(g * 128 + y, 8, stride=16), :] = tiles[y][half]
            for half in range(2):
                rows = tmp[half, pl.ds(pl.multiple_of(g * 128, 128), 128), :]
                store(g, half, rows.reshape(8, LY, 128))
            return 0

        lax.fori_loop(0, 4, body, 0)

    def store_rho(g, half, value):
        rho[pl.ds(H + 8 * g, 8), H : H + LY, half * 128 : half * 128 + 128] = value

    def store_vel(g, half, value):
        vel[pl.ds(8 * g, 8), :, half * 128 : half * 128 + 128] = value

    for c in xd:
        c.wait_recv()
    to_pencil(gotd, store_rho)

    def pack(i, _):
        sy[0, i, 0:4, :] = rho[H + i, H + 12 : H + 16, :]
        sy[0, i, 4:8, :] = rho[H + 16 + i, H + 12 : H + 16, :]
        sy[1, i, 0:4, :] = rho[H + i, H : H + 4, :]
        sy[1, i, 4:8, :] = rho[H + 16 + i, H : H + 4, :]
        return 0

    lax.fori_loop(0, 16, pack, 0)
    rho_halo = {
        "py_up": remote(sy.at[0], hy.at[0], dh_s.at[0], dh_r.at[0], sides["py_up"][2]),
        "py_down": remote(sy.at[1], hy.at[1], dh_s.at[1], dh_r.at[1], sides["py_down"][2]),
        "px_up": remote(rho.at[pl.ds(H + LX - 4, 4), pl.ds(H, LY), :], rho.at[pl.ds(H - 4, 4), pl.ds(H, LY), :], dh_s.at[2], dh_r.at[2], sides["px_up"][2]),
        "px_down": remote(rho.at[pl.ds(H, 4), pl.ds(H, LY), :], rho.at[pl.ds(H + LX, 4), pl.ds(H, LY), :], dh_s.at[3], dh_r.at[3], sides["px_down"][2]),
    }
    start_sides(rho_halo)

    agv[2].wait_recv()
    agv[3].start()
    agv[6].wait_recv()
    agv[5].start()
    serve_v(2, 6)

    def depth_part(g, _):
        block = rho[pl.ds(H + 8 * g, 8), H : H + LY, :].reshape(8 * LY, LZ)
        scale = 2.0 / (block + pltpu.roll(block, LZ - 1, 1))
        rows = pl.ds(8 * g, 8)
        for f in range(2):
            flux = fz[f, rows].reshape(8 * LY, LZ) * scale
            lap[f, rows] = dot(flux, dzb[...]).reshape(8, LY, LZ)
        return 0

    lax.fori_loop(0, 4, depth_part, 0)

    agv[3].wait_recv()
    agv[4].start()
    agv[5].wait_recv()
    agv[0].start()
    serve_v(3, 5)

    wait_sides(halos[1])
    forward_xy(1)

    agv[4].wait_recv()
    agv[0].wait_recv()
    serve_v(4)

    wait_sides(rho_halo)

    @pl.when(py > 0)
    def _():
        def body(i, _):
            rho[H + i, H - 4 : H, :] = hy[0, i, 0:4, :]
            rho[H + 16 + i, H - 4 : H, :] = hy[0, i, 4:8, :]
            return 0

        lax.fori_loop(0, 16, body, 0)

    @pl.when(py < NPY - 1)
    def _():
        def body(i, _):
            rho[H + i, H + LY : H + LY + 4, :] = hy[1, i, 0:4, :]
            rho[H + 16 + i, H + LY : H + LY + 4, :] = hy[1, i, 4:8, :]
            return 0

        lax.fori_loop(0, 16, body, 0)

    def flux_x(k, _):
        face = px * LX + k - 4
        two = jnp.where((face >= 0) & (face <= NPX * LX - 2), 2.0, 0.0)
        scale = two / (rho[k + 4, H : H + LY, :] + rho[k + 5, H : H + LY, :])
        for f in range(2):
            fx[f, k] = fx[f, k] * scale
        return 0

    lax.fori_loop(0, LX + 7, flux_x, 0)

    rows_y = lax.broadcasted_iota(jnp.int32, (LY + 2 * H, LZ), 0) - H
    face_y = rows_y + py * LY
    open_y = (rows_y >= -4) & (rows_y < LY + 3) & (face_y >= 0) & (face_y <= NPY * LY - 2)

    def flux_y(i, _):
        line = rho[H + i]
        scale = jnp.where(open_y, 2.0 / (line + pltpu.roll(line, LY + 2 * H - 1, 0)), 0.0)
        for f in range(2):
            fy[f, i] = fy[f, i] * scale
        return 0

    lax.fori_loop(0, LX, flux_y, 0)

    def laplacian(f, g):
        block = fy[f, pl.ds(8 * g, 8)].reshape(8 * (LY + 2 * H), LZ)
        total = lap[f, pl.ds(8 * g, 8)] + dot(myb[...], block).reshape(8, LY, LZ)
        for r, weight in enumerate(COEFS, 1):
            total = total + weight * (fx[f, pl.ds(8 * g + 3 + r, 8)] - fx[f, pl.ds(8 * g + 4 - r, 8)])
        return total

    for c in xv:
        c.wait_recv()
    to_pencil(gotv, store_vel)

    cell_s = src_cell[0]
    amp = src_amp[0]
    shape = (8, LY, LZ)
    iota_x = lax.broadcasted_iota(jnp.int32, shape, 0)
    iota_y = lax.broadcasted_iota(jnp.int32, shape, 1)
    iota_z = lax.broadcasted_iota(jnp.int32, shape, 2)
    flat = ((iota_x + px * LX) * (NPY * LY) + iota_y + py * LY) * LZ + iota_z

    def source_field(g, _):
        rows = pl.ds(8 * g, 8)
        v = vel[rows]
        step = COURANT2 * (rho[pl.ds(H + 8 * g, 8), H : H + LY, :] * v * v) * laplacian(0, g)
        step = step - jnp.where(flat + g * (8 * NPY * LY * LZ) == cell_s, amp, 0.0)
        nx[0, rows] = nx[0, rows] + step
        value = (2.0 / v) * u[1, pl.ds(H + 8 * g, 8), H : H + LY, :] * step
        for half in range(2):
            tmp[half, pl.ds(pl.multiple_of(g * 128, 128), 128), :] = value[:, :, half * 128 : half * 128 + 128].reshape(128, 128)
        tiles = []
        for y in range(LY):
            tiles.append([tmp[half, pl.ds(g * 128 + y, 8, stride=16), :] for half in range(2)])
        tiles = swap_groups(tiles)
        for m in range(BLOCKS):
            for half in range(2):
                contrib[m, pl.ds(pl.multiple_of(8 * g, 8), 8), half * 128 : half * 128 + 128] = tiles[m][half]
        return 0

    lax.fori_loop(0, 4, source_field, 0)
    out_f = pltpu.make_async_copy(nx.at[0], fwd_out, out_sem.at[0])
    out_f.start()

    xg = {}
    for d in (4, 3, 5, 2, 6, 1, 7, 0):
        for e in range(1, NX):
            owner = lax.rem(gy + NY - d, NY) * NX + lax.rem(gx + e, NX)
            gst[e - 1, d] = contrib[tbl_s[1, my_col, owner]]
            c = remote(gst.at[e - 1, d], grecv.at[e - 1, d], xg_s.at[e - 1, d], xg_r.at[e - 1, d], along_x(e))
            c.start()
            xg[e, d] = c

    def adjoint_field(g, _):
        rows = pl.ds(8 * g, 8)
        v = vel[rows]
        step = COURANT2 * (rho[pl.ds(H + 8 * g, 8), H : H + LY, :] * v * v) * laplacian(1, g)
        nx[1, rows] = nx[1, rows] + step
        return 0

    lax.fori_loop(0, 4, adjoint_field, 0)
    out_a = pltpu.make_async_copy(nx.at[1], adj_out, out_sem.at[1])
    out_a.start()

    def collect(d):
        for e in range(1, NX):
            xg[e, d].wait_recv()
        values = [contrib[tbl_s[1, my_col, owner_at(d)]]] + [grecv[NX - j - 1, d] for j in range(1, NX)]
        picks = [within_of(j, d) for j in range(NX)]
        for w in range(HELD):
            total = jnp.zeros((LX, LZ), jnp.float32)
            for j in range(NX):
                total = total + jnp.where(picks[j] == w + 1, values[j], 0.0)
            part[d][w] = total

    halves = (pl.ds(0, 2), pl.ds(2, 2))

    def send(src, slot, sem, target):
        c = remote(src, rs.at[slot], rs_s.at[sem], rs_r.at[sem], target)
        c.start()
        return c

    collect(4)
    m3 = remote(p4.at[halves[0]], rs.at[3, halves[0]], rs_s.at[3], rs_r.at[3], down)
    q5 = remote(p4.at[halves[1]], rs.at[5, halves[1]], rs_s.at[5], rs_r.at[5], up)
    m3.start()
    q5.start()
    collect(3)
    collect(5)
    m3.wait_recv()
    p3[0:2] = p3[0:2] + rs[3, 0:2]
    m2 = send(p3, 2, 2, down)
    q5.wait_recv()
    p5[2:4] = p5[2:4] + rs[5, 2:4]
    q6 = send(p5, 6, 6, up)
    collect(2)
    collect(6)
    m2.wait_recv()
    p2[...] = p2[...] + rs[2]
    m1 = send(p2, 1, 1, down)
    q6.wait_recv()
    p6[...] = p6[...] + rs[6]
    q7 = send(p6, 7, 7, up)
    collect(1)
    collect(7)
    m1.wait_recv()
    p1[...] = p1[...] + rs[1]
    m0 = send(p1, 0, 0, down)
    q7.wait_recv()
    p7[...] = p7[...] + rs[7]
    q0 = send(p7, 4, 4, up)
    collect(0)
    loads[6].wait()
    p0[...] = p0[...] + rs[8]
    m0.wait_recv()
    q0.wait_recv()
    p0[...] = p0[...] + (rs[0] + rs[4])
    out_g = pltpu.make_async_copy(p0, grad_out, out_sem.at[2])
    out_g.start()

    for c in col_copies + xd + xv + list(xg.values()) + list(agd.values()) + list(agv.values()):
        c.wait_send()
    for c in (m3, q5, m2, q6, m1, q7, m0, q0):
        c.wait_send()
    finish_sides(halos[0])
    finish_sides(halos[1])
    finish_sides(rho_halo)
    out_f.wait()
    out_a.wait()
    out_g.wait()


def shards(
    fwd_now,
    fwd_next,
    adj_now,
    adj_next,
    velocity,
    density,
    gradient_in,
    block_home,
    aperture_col,
    source_cell,
    source_amp,
    receiver_cell,
    receiver_residual,
):
    f32, i32 = jnp.float32, jnp.int32
    any_space = pl.BlockSpec(memory_space=pl.ANY)
    vmem = pl.BlockSpec(memory_space=pltpu.VMEM)
    smem = pl.BlockSpec(memory_space=pltpu.SMEM)
    pencil = (LX, LY, LZ)
    blocks = (HELD, LX, LZ)
    V = pltpu.VMEM
    D = pltpu.SemaphoreType.DMA
    scratch = [
        V((2, LX + 2 * H, LY + 2 * H, LZ), f32),
        V((2,) + pencil, f32),
        V((2, LX + 8, LY, LZ), f32),
        V((2, LX, LY + 2 * H, LZ), f32),
        V((2,) + pencil, f32),
        V((2,) + pencil, f32),
        V((LX + 2 * H, LY + 2 * H, LZ), f32),
        V(pencil, f32),
    ]
    scratch += [V(blocks, f32) for _ in range(16)]
    scratch += [
        V((NX - 1, NY, LX, LZ), f32),
        V((NX - 1, NY, LX, LZ), f32),
        V((NX * NY, LX, LZ), f32),
        V((NX * NY, LX, LZ), f32),
        V((2, LX * LY, 128), f32),
        V((2, 16, 8, LZ), f32),
        V((2, 16, 8, LZ), f32),
        V((BLOCKS, LX, LZ), f32),
        V((NX - 1, NY, LX, LZ), f32),
        V((NX - 1, NY, LX, LZ), f32),
    ]
    scratch += [V(blocks, f32) for _ in range(8)]
    scratch += [
        V((9,) + blocks, f32),
        V((256, 256), f32),
        V((256, 256), f32),
        V((256, 256), f32),
        V((128, 256), f32),
        V((2, 8, 128), i32),
        pltpu.SMEM((2, 8, 128), i32),
        V((8, 128), i32),
        V((NX - 1, 8, 128), i32),
        pltpu.SMEM((NX - 1, 8, 128), i32),
        D((9,)),
        D((8,)), D((8,)), D((8,)), D((8,)),
        D((3, 8)), D((3, 8)), D((3, 8)), D((3, 8)), D((3, 8)), D((3, 8)),
        D((8,)), D((8,)),
        D((2, 4)), D((2, 4)),
        D((4,)), D((4,)),
        D((3,)), D((3,)),
        D((3,)),
    ]
    fwd, adj, grad = pl.pallas_call(
        kernel,
        out_shape=(
            jax.ShapeDtypeStruct(pencil, f32),
            jax.ShapeDtypeStruct(pencil, f32),
            jax.ShapeDtypeStruct(blocks, f32),
        ),
        in_specs=[any_space] * 7 + [vmem, smem, smem, smem, smem, vmem, vmem],
        out_specs=(any_space, any_space, any_space),
        scratch_shapes=scratch,
        compiler_params=pltpu.CompilerParams(
            collective_id=0, has_side_effects=True, vmem_limit_bytes=48 * 2**20
        ),
        name="wave_step",
    )(
        fwd_now[0], adj_now[0], fwd_next[0], adj_next[0], velocity, density, gradient_in,
        block_home, block_home, aperture_col, source_cell, source_amp, receiver_cell, receiver_residual,
    )
    return fwd[None], adj[None], grad


def solution(mesh):
    in_specs = (
        P("shot", "px", "py", None),
        P("shot", "px", "py", None),
        P("shot", "px", "py", None),
        P("shot", "px", "py", None),
        P("shot", "px", "py"),
        P("shot", "px", "py"),
        P("shot", "px", "py"),
        P(),
        P("shot"),
        P("shot"),
        P("shot"),
        P("shot", None),
        P("shot", None),
    )
    out_specs = (P("shot", "px", "py", None), P("shot", "px", "py", None), P("shot", "px", "py"))
    return jax.shard_map(shards, mesh=mesh, in_specs=in_specs, out_specs=out_specs, check_vma=False)
```

```python
import functools

import jax
import jax.numpy as jnp
from jax import lax
from jax.experimental import pallas as pl
from jax.experimental.pallas import tpu as pltpu
from jax.sharding import PartitionSpec as P

COEFS = (1225.0 / 1024.0, -245.0 / 3072.0, 49.0 / 5120.0, -5.0 / 7168.0)
COURANT2 = 0.01
MESH = pl.DeviceIdType.MESH
HIGHEST = lax.Precision.HIGHEST

LX, LY, LZ = 32, 16, 256
NY, NX = 8, 4
NPX, NPY = 4, 4
BLOCKS, HELD, BZ = 16, 4, 16
H = 8


def dot(a, b):
    return jnp.dot(a, b, precision=HIGHEST, preferred_element_type=jnp.float32)


def band(delta, pairs):
    total = jnp.zeros(delta.shape, jnp.float32)
    for offset, weight in pairs:
        total = jnp.where(delta == offset, jnp.float32(weight), total)
    return total


FORWARD = tuple((r, c) for r, c in enumerate(COEFS, 1)) + tuple((1 - r, -c) for r, c in enumerate(COEFS, 1))
BACKWARD = tuple((r - 1, c) for r, c in enumerate(COEFS, 1)) + tuple((-r, -c) for r, c in enumerate(COEFS, 1))


def swap_groups(tiles):
    lane = lax.broadcasted_iota(jnp.int32, (8, 128), 1)
    tiles = [list(t) for t in tiles]
    for a in range(8):
        tiles[a][1], tiles[a + 8][0] = tiles[a + 8][0], tiles[a][1]
    for k in (4, 2, 1):
        set_bit = ((lane >> 4) & k) != 0
        for a in range(16):
            if a & k:
                continue
            for half in range(2):
                low, high = tiles[a][half], tiles[a + k][half]
                tiles[a][half] = jnp.where(set_bit, pltpu.roll(high, 16 * k, 1), low)
                tiles[a + k][half] = jnp.where(set_bit, high, pltpu.roll(low, 128 - 16 * k, 1))
    return tiles


def kernel(
    fwd_now, adj_now, fwd_next, adj_next, velocity, density, gradient_in,
    home, col, source, amplitude, receivers, residuals,
    fwd_out, adj_out, grad_out,
    u, nx, fx, fy, fz, lap, rho, vel,
    std, got0, got1, tmp, sy, hy,
    con, gst, grecv, gin, rs,
    dz, dzb, my, myb,
    tbl_v, tbl_s, colbuf, colrecv, cols_s,
    loc_sem, ag_s, ag_r, xd_s, xd_r, xg_s, xg_r,
    rs_s, rs_r, uh_s, uh_r, dh_s, dh_r, col_ss, col_rs, out_sem,
    home_v, home_s, col_s, src_cell, src_amp, rec_cell, rec_val, small_sem,
    note, notes, spike, nx_s, nx_r, ny_s, ny_r,
    *slots,
):
    chunk = [slots[8 * c : 8 * c + 8] for c in range(2)]
    part = slots[16:24]
    got = (got0, got1)
    place = {0: 0, 1: 1, 7: 2, 2: 3, 6: 4, 3: 5, 5: 6, 4: 7}
    shot = lax.axis_index("shot")
    px = lax.axis_index("px")
    py = lax.axis_index("py")
    gx = lax.rem(shot, NX)
    gy = shot // NX

    def along_x(e):
        return {"shot": gy * NX + lax.rem(gx + e, NX)}

    def along_y(e):
        return {"shot": lax.rem(gy + e, NY) * NX + gx}

    own = (density, velocity)
    own_loads = [pltpu.make_async_copy(own[c], chunk[c][0], loc_sem.at[c]) for c in range(2)]
    loads = [
        pltpu.make_async_copy(fwd_now, u.at[0, pl.ds(H, LX), pl.ds(H, LY), :], loc_sem.at[4]),
        pltpu.make_async_copy(adj_now, u.at[1, pl.ds(H, LX), pl.ds(H, LY), :], loc_sem.at[5]),
        pltpu.make_async_copy(fwd_next, nx.at[0], loc_sem.at[6]),
        pltpu.make_async_copy(adj_next, nx.at[1], loc_sem.at[7]),
        pltpu.make_async_copy(gradient_in, gin, loc_sem.at[8]),
    ]
    small = [
        pltpu.make_async_copy(src, dst, small_sem.at[i])
        for i, (src, dst) in enumerate(
            (
                (col, col_s), (home, home_v), (home, home_s), (source, src_cell),
                (amplitude, src_amp), (receivers, rec_cell), (residuals, rec_val),
            )
        )
    ]
    for c in small + own_loads + loads:
        c.start()

    def zero_rows(start):
        def body(i, _):
            u[0, H + i, start : start + H, :] = jnp.zeros((H, LZ), jnp.float32)
            u[1, H + i, start : start + H, :] = jnp.zeros((H, LZ), jnp.float32)
            return 0

        lax.fori_loop(0, LX, body, 0)

    def zero_slabs(start):
        def body(i, _):
            u[0, start + i, H : H + LY, :] = jnp.zeros((LY, LZ), jnp.float32)
            u[1, start + i, H : H + LY, :] = jnp.zeros((LY, LZ), jnp.float32)
            return 0

        lax.fori_loop(0, H, body, 0)

    barrier = pltpu.get_barrier_semaphore()
    for target in [along_y(1), along_y(NY - 1)] + [along_x(e) for e in range(1, NX)]:
        pl.semaphore_signal(barrier, inc=1, device_id=target, device_id_type=MESH)
    sides = {
        "px_up": (px < NPX - 1, px > 0, {"px": px + 1}),
        "px_down": (px > 0, px < NPX - 1, {"px": px - 1}),
        "py_up": (py < NPY - 1, py > 0, {"py": py + 1}),
        "py_down": (py > 0, py < NPY - 1, {"py": py - 1}),
    }
    for has, _, target in sides.values():

        @pl.when(has)
        def _():
            pl.semaphore_signal(barrier, inc=1, device_id=target, device_id_type=MESH)

    small[0].wait()
    my_col = col_s[0]
    colbuf[...] = jnp.zeros((8, 128), jnp.int32) + my_col

    present = [jnp.where(has, 1, 0) for has, _, _ in sides.values()]
    pl.semaphore_wait(barrier, NX + 1 + sum(present))

    def remote(src, dst, ss, rr, target):
        return pltpu.make_async_remote_copy(
            src_ref=src, dst_ref=dst, send_sem=ss, recv_sem=rr, device_id=target, device_id_type=MESH
        )

    col_copies = [
        remote(colbuf, colrecv.at[e - 1], col_ss.at[e - 1], col_rs.at[e - 1], along_x(e)) for e in range(1, NX)
    ]
    for c in col_copies:
        c.start()

    up, down = along_y(1), along_y(NY - 1)

    halves = (pl.ds(0, 2), pl.ds(2, 2))

    def gather(c):
        b, out = chunk[c], {}
        for d, src, target in (
            (1, own[c], up), (7, own[c], down), (2, b[1], up), (6, b[7], down),
            (3, b[2], up), (5, b[6], down), (4, b[3], up), (4, b[5], down),
        ):
            for w in range(2):
                if d == 4 and w != (0 if target is up else 1):
                    continue
                out[d, w] = remote(src.at[halves[w]], b[d].at[halves[w]], ag_s.at[c, d, w], ag_r.at[c, d, w], target)
        return out

    ag = [gather(c) for c in range(2)]

    def first(c):
        for w in range(2):
            ag[c][1, w].start()
            ag[c][7, w].start()

    def forward(c, d):
        for w in range(2):
            for k, to in ((d, d + 1), (NY - d, NY - d - 1)):
                ag[c][k, w].wait_recv()
                if (to, w) in ag[c] and not (to == 4 and w != (0 if k == 3 else 1)):
                    ag[c][to, w].start()

    first(0)

    def halo(f, field):
        s, r = uh_s, uh_r
        return {
            "py_up": remote(field.at[:, pl.ds(LY - H, H), :], u.at[f, pl.ds(H, LX), pl.ds(0, H), :], s.at[f, 0], r.at[f, 0], sides["py_up"][2]),
            "py_down": remote(field.at[:, pl.ds(0, H), :], u.at[f, pl.ds(H, LX), pl.ds(H + LY, H), :], s.at[f, 1], r.at[f, 1], sides["py_down"][2]),
            "px_up": remote(field.at[pl.ds(LX - H, H)], u.at[f, pl.ds(0, H), pl.ds(H, LY), :], s.at[f, 2], r.at[f, 2], sides["px_up"][2]),
            "px_down": remote(field.at[pl.ds(0, H)], u.at[f, pl.ds(H + LX, H), pl.ds(H, LY), :], s.at[f, 3], r.at[f, 3], sides["px_down"][2]),
        }

    def start_sides(copies):
        for name, c in copies.items():
            pl.when(sides[name][0])(c.start)

    def wait_sides(copies):
        for name, c in copies.items():
            pl.when(sides[name][1])(c.wait_recv)

    def finish_sides(copies):
        for name, c in copies.items():
            pl.when(sides[name][0])(c.wait_send)

    halos = [halo(0, fwd_now), halo(1, adj_now)]
    start_sides(halos[0])
    start_sides(halos[1])
    small[1].wait()
    small[2].wait()
    lane8 = lax.broadcasted_iota(jnp.int32, (8, 128), 1)
    within = jnp.zeros((8, 128), jnp.int32)
    depth_of = jnp.zeros((8, 128), jnp.int32)
    for m in range(BLOCKS):
        h = home_v[:, m : m + 1]
        hit = (h >> 2) == lane8
        within = jnp.where(hit, (h & 3) + 1, within)
        depth_of = jnp.where(hit, m, depth_of)
    tbl_v[0] = within
    tbl_v[1] = depth_of
    table_copy = pltpu.make_async_copy(tbl_v, tbl_s, loc_sem.at[9])
    table_copy.start()
    pl.when(py == 0)(lambda: zero_rows(0))
    pl.when(py == NPY - 1)(lambda: zero_rows(H + LY))
    pl.when(px == 0)(lambda: zero_slabs(0))
    pl.when(px == NPX - 1)(lambda: zero_slabs(H + LX))

    for c in col_copies:
        c.wait_recv()
    cols_copy = pltpu.make_async_copy(colrecv, cols_s, loc_sem.at[10])
    cols_copy.start()
    table_copy.wait()
    cols_copy.wait()
    cols = [my_col] + [cols_s[NX - j - 1, 0, 0] for j in range(1, NX)]

    def owner_at(d):
        return lax.rem(gy + NY - d, NY) * NX + gx

    def within_of(j, d):
        return tbl_s[0, cols[j], owner_at(d)]

    sent = [[], []]

    def serve(c, *slots_of):
        n, start = len(slots_of), place[slots_of[0]]
        for e in range(1, NX):
            for d in slots_of:
                std[c, e - 1, place[d]] = chunk[c][d][jnp.maximum(within_of(e, d) - 1, 0)]
            x = remote(
                std.at[c, e - 1, pl.ds(start, n)], got[c].at[pl.ds(e * NY + start, n)],
                xd_s.at[c, e - 1, start], xd_r.at[c, e - 1, start], along_x(e),
            )
            x.start()
            sent[c].append(x)
        for d in slots_of:
            got[c][place[d]] = chunk[c][d][jnp.maximum(within_of(0, d) - 1, 0)]

    def step(c, d):
        forward(c, d)
        serve(c, d, NY - d)

    def last(c):
        ag[c][4, 0].wait_recv()
        ag[c][4, 1].wait_recv()
        serve(c, 4)

    def place_of(m):
        owner = home_s[my_col, m] >> 2
        d = (gy - (owner >> 2)) & 7
        at = jnp.where(d == 0, 0, jnp.where(d <= 4, 2 * d - 1, 16 - 2 * d))
        return ((gx - (owner & 3)) & 3) * NY + at

    own_loads[0].wait()
    serve(0, 0)

    def build(i, _):
        start = pl.multiple_of(i * 32, 32)
        row = lax.broadcasted_iota(jnp.int32, (32, 256), 0) + start
        colm = lax.broadcasted_iota(jnp.int32, (32, 256), 1)
        forward = jnp.where(colm < LZ - 1, band(row - colm, FORWARD), 0.0)
        dz[pl.ds(start, 32), :] = forward
        dzb[pl.ds(start, 32), :] = band(row - colm, BACKWARD)
        same = (row >> 5) == (colm >> 5)
        my[pl.ds(start, 32), :] = jnp.where(same, band(colm - row, FORWARD), 0.0)
        return 0

    lax.fori_loop(0, 8, build, 0)

    def build_back(i, _):
        start = pl.multiple_of(i * 32, 32)
        row = lax.broadcasted_iota(jnp.int32, (32, 256), 0) + start
        colm = lax.broadcasted_iota(jnp.int32, (32, 256), 1)
        same = (row >> 4) == (colm >> 5)
        delta = ((colm & 31) - H) - (row & 15)
        myb[pl.ds(start, 32), :] = jnp.where(same, band(delta, BACKWARD), 0.0)
        return 0

    lax.fori_loop(0, 4, build_back, 0)

    step(0, 1)

    loads[0].wait()
    loads[1].wait()

    def forward_z(f):
        def body(g, _):
            block = u[f, pl.ds(H + 8 * g, 8), H : H + LY, :].reshape(8 * LY, LZ)
            fz[f, pl.ds(8 * g, 8)] = dot(block, dz[...]).reshape(8, LY, LZ)
            return 0

        lax.fori_loop(0, 4, body, 0)

    for c in small[3:]:
        c.wait()
    cell_s = src_cell[0]
    amp = src_amp[0]
    shape = (8, LY, LZ)
    iota_x = lax.broadcasted_iota(jnp.int32, shape, 0)
    iota_y = lax.broadcasted_iota(jnp.int32, shape, 1)
    iota_z = lax.broadcasted_iota(jnp.int32, shape, 2)
    flat = ((iota_x + px * LX) * (NPY * LY) + iota_y + py * LY) * LZ + iota_z
    note_x = [
        remote(note, notes.at[0, e], nx_s.at[e - 1], nx_r.at[e - 1], along_x(e)) for e in range(1, NX)
    ]
    note_y = {}
    for d, k, target in ((1, 0, up), (2, 1, up), (3, 2, up), (4, 3, up), (7, 0, down), (6, 7, down), (5, 6, down)):
        note_y[d] = remote(notes.at[k], notes.at[d], ny_s.at[d], ny_r.at[d], target)

    def write_note():
        def body(g, total):
            block = u[1, pl.ds(H + 8 * g, 8), H : H + LY, :]
            hit = jnp.where(flat + g * (8 * NPY * LY * LZ) == cell_s, block, 0.0)
            return total + jnp.sum(hit, axis=0)

        value = jnp.sum(lax.fori_loop(0, 4, body, jnp.zeros((LY, LZ), jnp.float32))) * amp
        x, y, z = (cell_s >> 14) - px * LX, ((cell_s >> 8) & 63) - py * LY, cell_s & 255
        mine = (x >= 0) & (x < LX) & (y >= 0) & (y < LY)
        block = home_s[my_col, z >> 4]
        at = jnp.where(mine, block * (LX * LZ) + x * LZ + y * BZ + (z & 15), -1)
        row = lax.broadcasted_iota(jnp.int32, (8, 128), 0)
        tile = jnp.where(row == 0, at.astype(jnp.float32), value)
        note[...] = tile
        notes[0, 0] = tile
        for c in note_x:
            c.start()

    forward_z(0)
    step(0, 2)
    write_note()
    step(0, 3)
    first(1)
    for c in note_x:
        c.wait_recv()
    note_y[1].start()
    note_y[7].start()
    forward_z(1)

    cell = rec_cell[...]
    cell_x = (cell >> 14) - px * LX
    cell_y = ((cell >> 8) & 63) - py * LY
    cell_z = cell & 255
    here = (cell_x >= 0) & (cell_x < LX) & (cell_y >= 0) & (cell_y < LY)
    spot = jnp.where(here, cell_x * LY + cell_y, -1)
    by_depth = jnp.where(lax.broadcasted_iota(jnp.int32, (LZ, 256), 0) == cell_z, rec_val[...], 0.0)
    loads[2].wait()
    loads[3].wait()

    def bases(g, _):
        start = pl.multiple_of(g * 128, 128)
        at = (lax.broadcasted_iota(jnp.int32, (128, 256), 0) + start == spot).astype(jnp.float32)
        added = lax.dot_general(
            at, by_depth, (((1,), (1,)), ((), ())), precision=HIGHEST, preferred_element_type=jnp.float32
        ).reshape(8, LY, LZ)
        rows = pl.ds(8 * g, 8)
        nx[0, rows] = 2.0 * u[0, pl.ds(H + 8 * g, 8), H : H + LY, :] - nx[0, rows]
        nx[1, rows] = 2.0 * u[1, pl.ds(H + 8 * g, 8), H : H + LY, :] - nx[1, rows] + added
        return 0

    lax.fori_loop(0, 4, bases, 0)

    last(0)
    own_loads[1].wait()
    serve(1, 0)

    def forward_xy(f):
        def body_x(k, _):
            total = None
            for r, weight in enumerate(COEFS, 1):
                term = weight * (u[f, k + 4 + r, H : H + LY, :] - u[f, k + 5 - r, H : H + LY, :])
                total = term if total is None else total + term
            fx[f, k] = total
            return 0

        lax.fori_loop(0, LX + 7, body_x, 0)

        def body_y(g, _):
            block = u[f, pl.ds(H + 8 * g, 8)].reshape(8 * (LY + 2 * H), LZ)
            fy[f, pl.ds(8 * g, 8)] = dot(my[...], block).reshape(8, LY + 2 * H, LZ)
            return 0

        lax.fori_loop(0, 4, body_y, 0)

    wait_sides(halos[0])
    forward_xy(0)
    step(1, 1)

    def to_pencil(c, store):
        for x in sent[c]:
            x.wait_recv()
        places = [place_of(m) for m in range(BLOCKS)]

        def body(k, _):
            tiles = []
            for m in range(BLOCKS):
                slab = got[c][places[m], pl.ds(pl.multiple_of(8 * k, 8), 8), :]
                tiles.append([slab[:, :128], slab[:, 128:]])
            tiles = swap_groups(tiles)
            for y in range(LY):
                for half in range(2):
                    tmp[half, pl.ds(k * 128 + y, 8, stride=16), :] = tiles[y][half]
            for half in range(2):
                rows = tmp[half, pl.ds(pl.multiple_of(k * 128, 128), 128), :]
                store(k, half, rows.reshape(8, LY, 128))
            return 0

        lax.fori_loop(0, 4, body, 0)

    def store_rho(g, half, value):
        rho[pl.ds(H + 8 * g, 8), H : H + LY, half * 128 : half * 128 + 128] = value

    def store_vel(g, half, value):
        vel[pl.ds(8 * g, 8), :, half * 128 : half * 128 + 128] = value

    to_pencil(0, store_rho)

    def pack(i, _):
        sy[0, i, 0:4, :] = rho[H + i, H + 12 : H + 16, :]
        sy[0, i, 4:8, :] = rho[H + 16 + i, H + 12 : H + 16, :]
        sy[1, i, 0:4, :] = rho[H + i, H : H + 4, :]
        sy[1, i, 4:8, :] = rho[H + 16 + i, H : H + 4, :]
        return 0

    lax.fori_loop(0, 16, pack, 0)
    rho_halo = {
        "py_up": remote(sy.at[0], hy.at[0], dh_s.at[0], dh_r.at[0], sides["py_up"][2]),
        "py_down": remote(sy.at[1], hy.at[1], dh_s.at[1], dh_r.at[1], sides["py_down"][2]),
        "px_up": remote(rho.at[pl.ds(H + LX - 4, 4), pl.ds(H, LY), :], rho.at[pl.ds(H - 4, 4), pl.ds(H, LY), :], dh_s.at[2], dh_r.at[2], sides["px_up"][2]),
        "px_down": remote(rho.at[pl.ds(H, 4), pl.ds(H, LY), :], rho.at[pl.ds(H + LX, 4), pl.ds(H, LY), :], dh_s.at[3], dh_r.at[3], sides["px_down"][2]),
    }
    start_sides(rho_halo)
    step(1, 2)
    for d, k in ((1, 2), (7, 6)):
        note_y[d].wait_recv()
        note_y[k].start()

    def depth_part(f, g):
        block = rho[pl.ds(H + 8 * g, 8), H : H + LY, :].reshape(8 * LY, LZ)
        scale = 2.0 / (block + pltpu.roll(block, LZ - 1, 1))
        rows = pl.ds(8 * g, 8)
        flux = fz[f, rows].reshape(8 * LY, LZ) * scale
        lap[f, rows] = dot(flux, dzb[...]).reshape(8, LY, LZ)

    def depth_parts(f):
        def body(g, _):
            depth_part(f, g)
            return 0

        lax.fori_loop(0, 4, body, 0)

    depth_parts(0)
    step(1, 3)
    for d, k in ((2, 3), (6, 5)):
        note_y[d].wait_recv()
        note_y[k].start()

    wait_sides(halos[1])
    forward_xy(1)
    depth_parts(1)
    note_y[3].wait_recv()
    note_y[4].start()
    last(1)

    wait_sides(rho_halo)

    @pl.when(py > 0)
    def _():
        def body(i, _):
            rho[H + i, H - 4 : H, :] = hy[0, i, 0:4, :]
            rho[H + 16 + i, H - 4 : H, :] = hy[0, i, 4:8, :]
            return 0

        lax.fori_loop(0, 16, body, 0)

    @pl.when(py < NPY - 1)
    def _():
        def body(i, _):
            rho[H + i, H + LY : H + LY + 4, :] = hy[1, i, 0:4, :]
            rho[H + 16 + i, H + LY : H + LY + 4, :] = hy[1, i, 4:8, :]
            return 0

        lax.fori_loop(0, 16, body, 0)

    def flux_x(f):
        def body(k, _):
            face = px * LX + k - 4
            open_x = (face >= 0) & (face <= NPX * LX - 2)
            scale = jnp.where(open_x, 2.0 / (rho[k + 4, H : H + LY, :] + rho[k + 5, H : H + LY, :]), 0.0)
            fx[f, k] = fx[f, k] * scale
            return 0

        lax.fori_loop(0, LX + 7, body, 0)

    rows_y = lax.broadcasted_iota(jnp.int32, (LY + 2 * H, LZ), 0) - H
    face_y = rows_y + py * LY
    open_y = (rows_y >= -4) & (rows_y < LY + 3) & (face_y >= 0) & (face_y <= NPY * LY - 2)

    def flux_y(f):
        def body(i, _):
            line = rho[H + i]
            scale = jnp.where(open_y, 2.0 / (line + pltpu.roll(line, LY + 2 * H - 1, 0)), 0.0)
            fy[f, i] = fy[f, i] * scale
            return 0

        lax.fori_loop(0, LX, body, 0)

    flux_x(0)
    flux_y(0)

    def laplacian(f, g):
        block = fy[f, pl.ds(8 * g, 8)].reshape(8 * (LY + 2 * H), LZ)
        total = lap[f, pl.ds(8 * g, 8)] + dot(myb[...], block).reshape(8, LY, LZ)
        for r, weight in enumerate(COEFS, 1):
            total = total + weight * (fx[f, pl.ds(8 * g + 3 + r, 8)] - fx[f, pl.ds(8 * g + 4 - r, 8)])
        return total

    def source_field(g, _):
        rows = pl.ds(8 * g, 8)
        change = laplacian(0, g)
        lap[0, rows] = change
        value = change * u[1, pl.ds(H + 8 * g, 8), H : H + LY, :]
        for half in range(2):
            tmp[half, pl.ds(pl.multiple_of(g * 128, 128), 128), :] = value[:, :, half * 128 : half * 128 + 128].reshape(128, 128)
        tiles = []
        for y in range(LY):
            tiles.append([tmp[half, pl.ds(g * 128 + y, 8, stride=16), :] for half in range(2)])
        tiles = swap_groups(tiles)
        for m in range(BLOCKS):
            for half in range(2):
                con[m, pl.ds(pl.multiple_of(8 * g, 8), 8), half * 128 : half * 128 + 128] = tiles[m][half]
        return 0

    xg = {}

    lax.fori_loop(0, 4, source_field, 0)

    def send_back(*slots_of):
        n, start = len(slots_of), place[slots_of[0]]
        for e in range(1, NX):
            for d in slots_of:
                owner = lax.rem(gy + NY - d, NY) * NX + lax.rem(gx + e, NX)
                gst[e - 1, place[d]] = con[tbl_s[1, my_col, owner]]
            c = remote(
                gst.at[e - 1, pl.ds(start, n)], grecv.at[e - 1, pl.ds(start, n)],
                xg_s.at[e - 1, start], xg_r.at[e - 1, start], along_x(e),
            )
            c.start()
            xg[e, slots_of[0]] = c

    for group in ((4,), (3, 5), (2, 6), (1, 7), (0,)):
        send_back(*group)

    def scaled(g):
        v = vel[pl.ds(8 * g, 8)]
        return COURANT2 * (rho[pl.ds(H + 8 * g, 8), H : H + LY, :] * v * v)

    def update_source(g, _):
        rows = pl.ds(8 * g, 8)
        change = scaled(g) * lap[0, rows] - jnp.where(flat + g * (8 * NPY * LY * LZ) == cell_s, amp, 0.0)
        nx[0, rows] = nx[0, rows] + change
        return 0

    def update_adjoint(g, _):
        rows = pl.ds(8 * g, 8)
        nx[1, rows] = nx[1, rows] + scaled(g) * laplacian(1, g)
        return 0

    def sources_of(w):
        row = lax.broadcasted_iota(jnp.int32, (LX, 128), 0)
        lane = lax.broadcasted_iota(jnp.int32, (LX, 128), 1)
        cells = ((shot * HELD + w) * LX + row) * LZ + lane

        def body(r, totals):
            at = notes[r // NX, lax.rem(r, NX), 0:1, :].astype(jnp.int32)
            value = notes[r // NX, lax.rem(r, NX), 1:2, :]
            return tuple(
                total + jnp.where(cells + half * 128 == at, value, 0.0) for half, total in enumerate(totals)
            )

        zero = jnp.zeros((LX, 128), jnp.float32)
        totals = lax.fori_loop(0, NX * NY, body, (zero, zero))
        for half in range(2):
            spike[w, :, half * 128 : half * 128 + 128] = totals[half]

    def collect(*slots_of):
        for e in range(1, NX):
            xg[e, slots_of[0]].wait_recv()
        for d in slots_of:
            values = [con[tbl_s[1, my_col, owner_at(d)]]] + [grecv[NX - j - 1, place[d]] for j in range(1, NX)]
            picks = [within_of(j, d) for j in range(NX)]
            for w in range(HELD):
                total = None
                for j in range(NX):
                    term = jnp.where(picks[j] == w + 1, values[j], 0.0)
                    total = term if total is None else total + term
                part[d][w] = total

    ring = {}
    for d, to, target in ((4, 3, down), (3, 2, down), (2, 1, down), (1, 0, down), (4, 5, up), (5, 6, up), (6, 7, up), (7, 8, up)):
        for w in range(2):
            if d == 4 and w != (0 if to == 3 else 1):
                continue
            ring[to, w] = remote(
                part[d].at[halves[w]], rs.at[to, halves[w]], rs_s.at[to, w], rs_r.at[to, w], target
            )

    def add(d, w):
        ring[d, w].wait_recv()
        rows = slice(2 * w, 2 * w + 2)
        part[d][rows] = part[d][rows] + rs[d, rows]

    for d in (4, 5):
        note_y[d].wait_recv()
    for w in range(2):
        sources_of(w)
    flux_x(1)
    flux_y(1)
    collect(4)
    ring[3, 0].start()
    ring[5, 1].start()
    collect(3, 5)
    ring[2, 1].start()
    ring[6, 0].start()
    for w in range(2, HELD):
        sources_of(w)
    add(3, 0)
    ring[2, 0].start()
    add(5, 1)
    ring[6, 1].start()
    collect(2, 6)
    add(2, 1)
    ring[1, 1].start()
    add(6, 0)
    ring[7, 0].start()
    add(2, 0)
    ring[1, 0].start()
    add(6, 1)
    ring[7, 1].start()
    to_pencil(1, store_vel)
    collect(1, 7)
    add(1, 1)
    ring[0, 1].start()
    add(7, 0)
    ring[8, 0].start()
    add(1, 0)
    ring[0, 0].start()
    add(7, 1)
    ring[8, 1].start()
    collect(0)
    loads[4].wait()

    def settle(w, _):
        own_vel = chunk[1][0][w]
        gin[w] = gin[w] - (2.0 / own_vel) * spike[w]
        spike[w] = (2.0 * COURANT2) * (chunk[0][0][w] * own_vel)
        return 0

    lax.fori_loop(0, HELD, settle, 0)
    lax.fori_loop(0, 4, update_source, 0)
    out_f = pltpu.make_async_copy(nx.at[0], fwd_out, out_sem.at[0])
    out_f.start()
    lax.fori_loop(0, 4, update_adjoint, 0)
    out_a = pltpu.make_async_copy(nx.at[1], adj_out, out_sem.at[1])
    out_a.start()
    for w in (1, 0):
        ring[0, w].wait_recv()
        ring[8, 1 - w].wait_recv()
    for w in range(HELD):
        gin[w] = gin[w] + spike[w] * (part[0][w] + (rs[0, w] + rs[8, w]))
    out_g = pltpu.make_async_copy(gin, grad_out, out_sem.at[2])
    out_g.start()

    for c in col_copies + note_x + list(note_y.values()) + sent[0] + sent[1] + list(xg.values()) + list(ring.values()):
        c.wait_send()
    for copies in ag:
        for c in copies.values():
            c.wait_send()
    finish_sides(halos[0])
    finish_sides(halos[1])
    finish_sides(rho_halo)
    out_f.wait()
    out_a.wait()
    out_g.wait()


def shards(
    fwd_now,
    fwd_next,
    adj_now,
    adj_next,
    velocity,
    density,
    gradient_in,
    block_home,
    aperture_col,
    source_cell,
    source_amp,
    receiver_cell,
    receiver_residual,
):
    f32, i32 = jnp.float32, jnp.int32
    any_space = pl.BlockSpec(memory_space=pl.ANY)
    pencil = (LX, LY, LZ)
    blocks = (HELD, LX, LZ)
    V = pltpu.VMEM
    D = pltpu.SemaphoreType.DMA
    scratch = [
        V((2, LX + 2 * H, LY + 2 * H, LZ), f32),
        V((2,) + pencil, f32),
        V((2, LX + 8, LY, LZ), f32),
        V((2, LX, LY + 2 * H, LZ), f32),
        V((2,) + pencil, f32),
        V((2,) + pencil, f32),
        V((LX + 2 * H, LY + 2 * H, LZ), f32),
        V(pencil, f32),
    ]
    scratch += [
        V((2, NX - 1, NY, LX, LZ), f32),
        V((NX * NY, LX, LZ), f32),
        V((NX * NY, LX, LZ), f32),
        V((2, LX * LY, 128), f32),
        V((2, 16, 8, LZ), f32),
        V((2, 16, 8, LZ), f32),
        V((BLOCKS, LX, LZ), f32),
        V((NX - 1, NY, LX, LZ), f32),
        V((NX - 1, NY, LX, LZ), f32),
        V(blocks, f32),
        V((9,) + blocks, f32),
        V((256, 256), f32),
        V((256, 256), f32),
        V((256, 256), f32),
        V((128, 256), f32),
        V((2, 8, 128), i32),
        pltpu.SMEM((2, 8, 128), i32),
        V((8, 128), i32),
        V((NX - 1, 8, 128), i32),
        pltpu.SMEM((NX - 1, 8, 128), i32),
        D((11,)),
        D((2, 8, 2)), D((2, 8, 2)),
        D((2, 3, 8)), D((2, 3, 8)),
        D((3, 8)), D((3, 8)),
        D((9, 2)), D((9, 2)),
        D((2, 4)), D((2, 4)),
        D((4,)), D((4,)),
        D((3,)), D((3,)),
        D((3,)),
        V((8, 16), i32),
        pltpu.SMEM((8, 16), i32),
        pltpu.SMEM((1,), i32),
        pltpu.SMEM((1,), i32),
        pltpu.SMEM((1,), f32),
        V((1, 256), i32),
        V((1, 256), f32),
        D((7,)),
        V((8, 128), f32),
        V((NY, NX, 8, 128), f32),
        V(blocks, f32),
        D((3,)), D((3,)),
        D((8,)), D((8,)),
    ]
    scratch += [V(blocks, f32) for _ in range(24)]
    fwd, adj, grad = pl.pallas_call(
        kernel,
        out_shape=(
            jax.ShapeDtypeStruct(pencil, f32),
            jax.ShapeDtypeStruct(pencil, f32),
            jax.ShapeDtypeStruct(blocks, f32),
        ),
        in_specs=[any_space] * 13,
        out_specs=(any_space, any_space, any_space),
        scratch_shapes=scratch,
        compiler_params=pltpu.CompilerParams(
            collective_id=0, has_side_effects=True, vmem_limit_bytes=62 * 2**20
        ),
        name="wave_step",
    )(
        fwd_now[0], adj_now[0], fwd_next[0], adj_next[0], velocity, density, gradient_in,
        block_home, aperture_col, source_cell, source_amp, receiver_cell, receiver_residual,
    )
    return fwd[None], adj[None], grad


def solution(mesh):
    in_specs = (
        P("shot", "px", "py", None),
        P("shot", "px", "py", None),
        P("shot", "px", "py", None),
        P("shot", "px", "py", None),
        P("shot", "px", "py"),
        P("shot", "px", "py"),
        P("shot", "px", "py"),
        P(),
        P("shot"),
        P("shot"),
        P("shot"),
        P("shot", None),
        P("shot", None),
    )
    out_specs = (P("shot", "px", "py", None), P("shot", "px", "py", None), P("shot", "px", "py"))
    return jax.shard_map(shards, mesh=mesh, in_specs=in_specs, out_specs=out_specs, check_vma=False)
```

```python
import functools

import jax
import jax.numpy as jnp
from jax import lax
from jax.experimental import pallas as pl
from jax.experimental.pallas import tpu as pltpu
from jax.sharding import PartitionSpec as P

COEFS = (1225.0 / 1024.0, -245.0 / 3072.0, 49.0 / 5120.0, -5.0 / 7168.0)
COURANT2 = 0.01
MESH = pl.DeviceIdType.MESH
HIGHEST = lax.Precision.HIGHEST

LX, LY, LZ = 32, 16, 256
NY, NX = 8, 4
NPX, NPY = 4, 4
BLOCKS, HELD, BZ = 16, 4, 16
H = 8


def dot(a, b):
    return jnp.dot(a, b, precision=HIGHEST, preferred_element_type=jnp.float32)


def band(delta, pairs):
    total = jnp.zeros(delta.shape, jnp.float32)
    for offset, weight in pairs:
        total = jnp.where(delta == offset, jnp.float32(weight), total)
    return total


FORWARD = tuple((r, c) for r, c in enumerate(COEFS, 1)) + tuple((1 - r, -c) for r, c in enumerate(COEFS, 1))
BACKWARD = tuple((r - 1, c) for r, c in enumerate(COEFS, 1)) + tuple((-r, -c) for r, c in enumerate(COEFS, 1))


def swap_groups(tiles):
    lane = lax.broadcasted_iota(jnp.int32, (8, 128), 1)
    tiles = [list(t) for t in tiles]
    for a in range(8):
        tiles[a][1], tiles[a + 8][0] = tiles[a + 8][0], tiles[a][1]
    for k in (4, 2, 1):
        set_bit = ((lane >> 4) & k) != 0
        for a in range(16):
            if a & k:
                continue
            for half in range(2):
                low, high = tiles[a][half], tiles[a + k][half]
                tiles[a][half] = jnp.where(set_bit, pltpu.roll(high, 16 * k, 1), low)
                tiles[a + k][half] = jnp.where(set_bit, high, pltpu.roll(low, 128 - 16 * k, 1))
    return tiles


def kernel(
    fwd_now, adj_now, fwd_next, adj_next, velocity, density, gradient_in,
    home, col, source, amplitude, receivers, residuals,
    fwd_out, adj_out, grad_out,
    u, nx, fx, fy, fz, lap, rho, vel,
    std, got0, got1, tmp, sy, hy,
    con, gst, grecv, gin, rs,
    dz, dzb, my, myb,
    tbl_v, tbl_s, colbuf, colrecv, cols_s,
    loc_sem, ag_s, ag_r, xd_s, xd_r, xg_s, xg_r,
    rs_s, rs_r, uh_s, uh_r, dh_s, dh_r, col_ss, col_rs, out_sem,
    home_v, home_s, col_s, src_cell, src_amp, rec_cell, rec_val, small_sem,
    note, notes, spike, nx_s, nx_r, ny_s, ny_r,
    *slots,
):
    chunk = [slots[8 * c : 8 * c + 8] for c in range(2)]
    part = slots[16:24]
    got = (got0, got1)
    place = {0: 0, 1: 1, 7: 2, 2: 3, 6: 4, 3: 5, 5: 6, 4: 7}
    shot = lax.axis_index("shot")
    px = lax.axis_index("px")
    py = lax.axis_index("py")
    gx = lax.rem(shot, NX)
    gy = shot // NX

    def along_x(e):
        return {"shot": gy * NX + lax.rem(gx + e, NX)}

    def along_y(e):
        return {"shot": lax.rem(gy + e, NY) * NX + gx}

    own = (density, velocity)
    own_loads = [pltpu.make_async_copy(own[c], chunk[c][0], loc_sem.at[c]) for c in range(2)]
    loads = [
        pltpu.make_async_copy(fwd_now, u.at[0, pl.ds(H, LX), pl.ds(H, LY), :], loc_sem.at[4]),
        pltpu.make_async_copy(adj_now, u.at[1, pl.ds(H, LX), pl.ds(H, LY), :], loc_sem.at[5]),
        pltpu.make_async_copy(fwd_next, nx.at[0], loc_sem.at[6]),
        pltpu.make_async_copy(adj_next, nx.at[1], loc_sem.at[7]),
        pltpu.make_async_copy(gradient_in, gin, loc_sem.at[8]),
    ]
    small = [
        pltpu.make_async_copy(src, dst, small_sem.at[i])
        for i, (src, dst) in enumerate(
            (
                (col, col_s), (home, home_v), (home, home_s), (source, src_cell),
                (amplitude, src_amp), (receivers, rec_cell), (residuals, rec_val),
            )
        )
    ]
    for c in small + own_loads + loads:
        c.start()

    def zero_rows(start):
        def body(i, _):
            u[0, H + i, start : start + H, :] = jnp.zeros((H, LZ), jnp.float32)
            u[1, H + i, start : start + H, :] = jnp.zeros((H, LZ), jnp.float32)
            return 0

        lax.fori_loop(0, LX, body, 0)

    def zero_slabs(start):
        def body(i, _):
            u[0, start + i, H : H + LY, :] = jnp.zeros((LY, LZ), jnp.float32)
            u[1, start + i, H : H + LY, :] = jnp.zeros((LY, LZ), jnp.float32)
            return 0

        lax.fori_loop(0, H, body, 0)

    barrier = pltpu.get_barrier_semaphore()
    for target in [along_y(1), along_y(NY - 1)] + [along_x(e) for e in range(1, NX)]:
        pl.semaphore_signal(barrier, inc=1, device_id=target, device_id_type=MESH)
    sides = {
        "px_up": (px < NPX - 1, px > 0, {"px": px + 1}),
        "px_down": (px > 0, px < NPX - 1, {"px": px - 1}),
        "py_up": (py < NPY - 1, py > 0, {"py": py + 1}),
        "py_down": (py > 0, py < NPY - 1, {"py": py - 1}),
    }
    for has, _, target in sides.values():

        @pl.when(has)
        def _():
            pl.semaphore_signal(barrier, inc=1, device_id=target, device_id_type=MESH)

    small[0].wait()
    my_col = col_s[0]
    colbuf[...] = jnp.zeros((8, 128), jnp.int32) + my_col

    present = [jnp.where(has, 1, 0) for has, _, _ in sides.values()]
    pl.semaphore_wait(barrier, NX + 1 + sum(present))

    def remote(src, dst, ss, rr, target):
        return pltpu.make_async_remote_copy(
            src_ref=src, dst_ref=dst, send_sem=ss, recv_sem=rr, device_id=target, device_id_type=MESH
        )

    col_copies = [
        remote(colbuf, colrecv.at[e - 1], col_ss.at[e - 1], col_rs.at[e - 1], along_x(e)) for e in range(1, NX)
    ]
    for c in col_copies:
        c.start()

    up, down = along_y(1), along_y(NY - 1)

    halves = (pl.ds(0, 2), pl.ds(2, 2))

    def gather(c):
        b, out = chunk[c], {}
        for d, src, target in (
            (1, own[c], up), (7, own[c], down), (2, b[1], up), (6, b[7], down),
            (3, b[2], up), (5, b[6], down), (4, b[3], up), (4, b[5], down),
        ):
            for w in range(2):
                if d == 4 and w != (0 if target is up else 1):
                    continue
                out[d, w] = remote(src.at[halves[w]], b[d].at[halves[w]], ag_s.at[c, d, w], ag_r.at[c, d, w], target)
        return out

    ag = [gather(c) for c in range(2)]

    def first(c):
        for w in range(2):
            ag[c][1, w].start()
            ag[c][7, w].start()

    def forward(c, d):
        for w in range(2):
            for k, to in ((d, d + 1), (NY - d, NY - d - 1)):
                ag[c][k, w].wait_recv()
                if (to, w) in ag[c] and not (to == 4 and w != (0 if k == 3 else 1)):
                    ag[c][to, w].start()

    first(0)

    def halo(f, field):
        s, r = uh_s, uh_r
        return {
            "py_up": remote(field.at[:, pl.ds(LY - H, H), :], u.at[f, pl.ds(H, LX), pl.ds(0, H), :], s.at[f, 0], r.at[f, 0], sides["py_up"][2]),
            "py_down": remote(field.at[:, pl.ds(0, H), :], u.at[f, pl.ds(H, LX), pl.ds(H + LY, H), :], s.at[f, 1], r.at[f, 1], sides["py_down"][2]),
            "px_up": remote(field.at[pl.ds(LX - H, H)], u.at[f, pl.ds(0, H), pl.ds(H, LY), :], s.at[f, 2], r.at[f, 2], sides["px_up"][2]),
            "px_down": remote(field.at[pl.ds(0, H)], u.at[f, pl.ds(H + LX, H), pl.ds(H, LY), :], s.at[f, 3], r.at[f, 3], sides["px_down"][2]),
        }

    def start_sides(copies):
        for name, c in copies.items():
            pl.when(sides[name][0])(c.start)

    def wait_sides(copies):
        for name, c in copies.items():
            pl.when(sides[name][1])(c.wait_recv)

    def finish_sides(copies):
        for name, c in copies.items():
            pl.when(sides[name][0])(c.wait_send)

    halos = [halo(0, fwd_now), halo(1, adj_now)]
    start_sides(halos[0])
    small[1].wait()
    small[2].wait()
    lane8 = lax.broadcasted_iota(jnp.int32, (8, 128), 1)
    within = jnp.zeros((8, 128), jnp.int32)
    depth_of = jnp.zeros((8, 128), jnp.int32)
    for m in range(BLOCKS):
        h = home_v[:, m : m + 1]
        hit = (h >> 2) == lane8
        within = jnp.where(hit, (h & 3) + 1, within)
        depth_of = jnp.where(hit, m, depth_of)
    tbl_v[0] = within
    tbl_v[1] = depth_of
    table_copy = pltpu.make_async_copy(tbl_v, tbl_s, loc_sem.at[9])
    table_copy.start()
    pl.when(py == 0)(lambda: zero_rows(0))
    pl.when(py == NPY - 1)(lambda: zero_rows(H + LY))
    pl.when(px == 0)(lambda: zero_slabs(0))
    pl.when(px == NPX - 1)(lambda: zero_slabs(H + LX))

    for c in col_copies:
        c.wait_recv()
    cols_copy = pltpu.make_async_copy(colrecv, cols_s, loc_sem.at[10])
    cols_copy.start()
    table_copy.wait()
    cols_copy.wait()
    cols = [my_col] + [cols_s[NX - j - 1, 0, 0] for j in range(1, NX)]

    def owner_at(d):
        return lax.rem(gy + NY - d, NY) * NX + gx

    def within_of(j, d):
        return tbl_s[0, cols[j], owner_at(d)]

    sent = [[], []]

    def serve(c, *slots_of):
        n, start = len(slots_of), place[slots_of[0]]
        for e in range(1, NX):
            for d in slots_of:
                std[c, e - 1, place[d]] = chunk[c][d][jnp.maximum(within_of(e, d) - 1, 0)]
            x = remote(
                std.at[c, e - 1, pl.ds(start, n)], got[c].at[pl.ds(e * NY + start, n)],
                xd_s.at[c, e - 1, start], xd_r.at[c, e - 1, start], along_x(e),
            )
            x.start()
            sent[c].append(x)
        for d in slots_of:
            got[c][place[d]] = chunk[c][d][jnp.maximum(within_of(0, d) - 1, 0)]

    def step(c, d):
        forward(c, d)
        serve(c, d, NY - d)

    def last(c):
        ag[c][4, 0].wait_recv()
        ag[c][4, 1].wait_recv()
        serve(c, 4)

    def place_of(m):
        owner = home_s[my_col, m] >> 2
        d = (gy - (owner >> 2)) & 7
        at = jnp.where(d == 0, 0, jnp.where(d <= 4, 2 * d - 1, 16 - 2 * d))
        return ((gx - (owner & 3)) & 3) * NY + at

    own_loads[0].wait()
    serve(0, 0)

    def build(i, _):
        start = pl.multiple_of(i * 32, 32)
        row = lax.broadcasted_iota(jnp.int32, (32, 256), 0) + start
        colm = lax.broadcasted_iota(jnp.int32, (32, 256), 1)
        forward = jnp.where(colm < LZ - 1, band(row - colm, FORWARD), 0.0)
        dz[pl.ds(start, 32), :] = forward
        dzb[pl.ds(start, 32), :] = band(row - colm, BACKWARD)
        same = (row >> 5) == (colm >> 5)
        my[pl.ds(start, 32), :] = jnp.where(same, band(colm - row, FORWARD), 0.0)
        return 0

    lax.fori_loop(0, 8, build, 0)

    def build_back(i, _):
        start = pl.multiple_of(i * 32, 32)
        row = lax.broadcasted_iota(jnp.int32, (32, 256), 0) + start
        colm = lax.broadcasted_iota(jnp.int32, (32, 256), 1)
        same = (row >> 4) == (colm >> 5)
        delta = ((colm & 31) - H) - (row & 15)
        myb[pl.ds(start, 32), :] = jnp.where(same, band(delta, BACKWARD), 0.0)
        return 0

    lax.fori_loop(0, 4, build_back, 0)

    step(0, 1)

    loads[0].wait()
    loads[1].wait()

    def forward_z(f):
        def body(g, _):
            block = u[f, pl.ds(H + 8 * g, 8), H : H + LY, :].reshape(8 * LY, LZ)
            fz[f, pl.ds(8 * g, 8)] = dot(block, dz[...]).reshape(8, LY, LZ)
            return 0

        lax.fori_loop(0, 4, body, 0)

    for c in small[3:]:
        c.wait()
    cell_s = src_cell[0]
    amp = src_amp[0]
    shape = (8, LY, LZ)
    iota_x = lax.broadcasted_iota(jnp.int32, shape, 0)
    iota_y = lax.broadcasted_iota(jnp.int32, shape, 1)
    iota_z = lax.broadcasted_iota(jnp.int32, shape, 2)
    flat = ((iota_x + px * LX) * (NPY * LY) + iota_y + py * LY) * LZ + iota_z
    note_x = [
        remote(note, notes.at[0, e], nx_s.at[e - 1], nx_r.at[e - 1], along_x(e)) for e in range(1, NX)
    ]
    note_y = {}
    for d, k, target in ((1, 0, up), (2, 1, up), (3, 2, up), (4, 3, up), (7, 0, down), (6, 7, down), (5, 6, down)):
        note_y[d] = remote(notes.at[k], notes.at[d], ny_s.at[d], ny_r.at[d], target)

    def write_note():
        def body(g, total):
            block = u[1, pl.ds(H + 8 * g, 8), H : H + LY, :]
            hit = jnp.where(flat + g * (8 * NPY * LY * LZ) == cell_s, block, 0.0)
            return total + jnp.sum(hit, axis=0)

        value = jnp.sum(lax.fori_loop(0, 4, body, jnp.zeros((LY, LZ), jnp.float32))) * amp
        x, y, z = (cell_s >> 14) - px * LX, ((cell_s >> 8) & 63) - py * LY, cell_s & 255
        mine = (x >= 0) & (x < LX) & (y >= 0) & (y < LY)
        block = home_s[my_col, z >> 4]
        at = jnp.where(mine, block * (LX * LZ) + x * LZ + y * BZ + (z & 15), -1)
        row = lax.broadcasted_iota(jnp.int32, (8, 128), 0)
        tile = jnp.where(row == 0, at.astype(jnp.float32), value)
        note[...] = tile
        notes[0, 0] = tile
        for c in note_x:
            c.start()

    forward_z(0)
    step(0, 2)
    write_note()
    step(0, 3)
    first(1)
    for c in note_x:
        c.wait_recv()
    note_y[1].start()
    note_y[7].start()
    forward_z(1)

    cell = rec_cell[...]
    cell_x = (cell >> 14) - px * LX
    cell_y = ((cell >> 8) & 63) - py * LY
    cell_z = cell & 255
    here = (cell_x >= 0) & (cell_x < LX) & (cell_y >= 0) & (cell_y < LY)
    spot = jnp.where(here, cell_x * LY + cell_y, -1)
    by_depth = jnp.where(lax.broadcasted_iota(jnp.int32, (LZ, 256), 0) == cell_z, rec_val[...], 0.0)
    loads[2].wait()
    loads[3].wait()

    def bases(g, _):
        start = pl.multiple_of(g * 128, 128)
        at = (lax.broadcasted_iota(jnp.int32, (128, 256), 0) + start == spot).astype(jnp.float32)
        added = lax.dot_general(
            at, by_depth, (((1,), (1,)), ((), ())), precision=HIGHEST, preferred_element_type=jnp.float32
        ).reshape(8, LY, LZ)
        rows = pl.ds(8 * g, 8)
        nx[0, rows] = 2.0 * u[0, pl.ds(H + 8 * g, 8), H : H + LY, :] - nx[0, rows]
        nx[1, rows] = 2.0 * u[1, pl.ds(H + 8 * g, 8), H : H + LY, :] - nx[1, rows] + added
        return 0

    lax.fori_loop(0, 4, bases, 0)

    last(0)
    own_loads[1].wait()
    serve(1, 0)

    def forward_xy(f):
        def body_x(k, _):
            total = None
            for r, weight in enumerate(COEFS, 1):
                term = weight * (u[f, k + 4 + r, H : H + LY, :] - u[f, k + 5 - r, H : H + LY, :])
                total = term if total is None else total + term
            fx[f, k] = total
            return 0

        lax.fori_loop(0, LX + 7, body_x, 0)

        def body_y(g, _):
            block = u[f, pl.ds(H + 8 * g, 8)].reshape(8 * (LY + 2 * H), LZ)
            fy[f, pl.ds(8 * g, 8)] = dot(my[...], block).reshape(8, LY + 2 * H, LZ)
            return 0

        lax.fori_loop(0, 4, body_y, 0)

    wait_sides(halos[0])
    forward_xy(0)
    step(1, 1)

    def to_pencil(c, store):
        for x in sent[c]:
            x.wait_recv()
        places = [place_of(m) for m in range(BLOCKS)]

        def body(k, _):
            tiles = []
            for m in range(BLOCKS):
                slab = got[c][places[m], pl.ds(pl.multiple_of(8 * k, 8), 8), :]
                tiles.append([slab[:, :128], slab[:, 128:]])
            tiles = swap_groups(tiles)
            for y in range(LY):
                for half in range(2):
                    tmp[half, pl.ds(k * 128 + y, 8, stride=16), :] = tiles[y][half]
            for half in range(2):
                rows = tmp[half, pl.ds(pl.multiple_of(k * 128, 128), 128), :]
                store(k, half, rows.reshape(8, LY, 128))
            return 0

        lax.fori_loop(0, 4, body, 0)

    def store_rho(g, half, value):
        rho[pl.ds(H + 8 * g, 8), H : H + LY, half * 128 : half * 128 + 128] = value

    def store_vel(g, half, value):
        vel[pl.ds(8 * g, 8), :, half * 128 : half * 128 + 128] = value

    to_pencil(0, store_rho)

    def pack(i, _):
        sy[0, i, 0:4, :] = rho[H + i, H + 12 : H + 16, :]
        sy[0, i, 4:8, :] = rho[H + 16 + i, H + 12 : H + 16, :]
        sy[1, i, 0:4, :] = rho[H + i, H : H + 4, :]
        sy[1, i, 4:8, :] = rho[H + 16 + i, H : H + 4, :]
        return 0

    lax.fori_loop(0, 16, pack, 0)
    rho_halo = {
        "py_up": remote(sy.at[0], hy.at[0], dh_s.at[0], dh_r.at[0], sides["py_up"][2]),
        "py_down": remote(sy.at[1], hy.at[1], dh_s.at[1], dh_r.at[1], sides["py_down"][2]),
        "px_up": remote(rho.at[pl.ds(H + LX - 4, 4), pl.ds(H, LY), :], rho.at[pl.ds(H - 4, 4), pl.ds(H, LY), :], dh_s.at[2], dh_r.at[2], sides["px_up"][2]),
        "px_down": remote(rho.at[pl.ds(H, 4), pl.ds(H, LY), :], rho.at[pl.ds(H + LX, 4), pl.ds(H, LY), :], dh_s.at[3], dh_r.at[3], sides["px_down"][2]),
    }
    start_sides(rho_halo)
    step(1, 2)
    for d, k in ((1, 2), (7, 6)):
        note_y[d].wait_recv()
        note_y[k].start()

    def depth_part(f, g):
        block = rho[pl.ds(H + 8 * g, 8), H : H + LY, :].reshape(8 * LY, LZ)
        scale = 2.0 / (block + pltpu.roll(block, LZ - 1, 1))
        rows = pl.ds(8 * g, 8)
        flux = fz[f, rows].reshape(8 * LY, LZ) * scale
        lap[f, rows] = dot(flux, dzb[...]).reshape(8, LY, LZ)

    def depth_parts(f):
        def body(g, _):
            depth_part(f, g)
            return 0

        lax.fori_loop(0, 4, body, 0)

    depth_parts(0)
    step(1, 3)
    for d, k in ((2, 3), (6, 5)):
        note_y[d].wait_recv()
        note_y[k].start()

    note_y[3].wait_recv()
    note_y[4].start()
    last(1)

    wait_sides(rho_halo)
    start_sides(halos[1])

    @pl.when(py > 0)
    def _():
        def body(i, _):
            rho[H + i, H - 4 : H, :] = hy[0, i, 0:4, :]
            rho[H + 16 + i, H - 4 : H, :] = hy[0, i, 4:8, :]
            return 0

        lax.fori_loop(0, 16, body, 0)

    @pl.when(py < NPY - 1)
    def _():
        def body(i, _):
            rho[H + i, H + LY : H + LY + 4, :] = hy[1, i, 0:4, :]
            rho[H + 16 + i, H + LY : H + LY + 4, :] = hy[1, i, 4:8, :]
            return 0

        lax.fori_loop(0, 16, body, 0)

    def flux_x(f):
        def body(k, _):
            face = px * LX + k - 4
            open_x = (face >= 0) & (face <= NPX * LX - 2)
            scale = jnp.where(open_x, 2.0 / (rho[k + 4, H : H + LY, :] + rho[k + 5, H : H + LY, :]), 0.0)
            fx[f, k] = fx[f, k] * scale
            return 0

        lax.fori_loop(0, LX + 7, body, 0)

    rows_y = lax.broadcasted_iota(jnp.int32, (LY + 2 * H, LZ), 0) - H
    face_y = rows_y + py * LY
    open_y = (rows_y >= -4) & (rows_y < LY + 3) & (face_y >= 0) & (face_y <= NPY * LY - 2)

    def flux_y(f):
        def body(i, _):
            line = rho[H + i]
            scale = jnp.where(open_y, 2.0 / (line + pltpu.roll(line, LY + 2 * H - 1, 0)), 0.0)
            fy[f, i] = fy[f, i] * scale
            return 0

        lax.fori_loop(0, LX, body, 0)

    flux_x(0)
    flux_y(0)

    def laplacian(f, g):
        block = fy[f, pl.ds(8 * g, 8)].reshape(8 * (LY + 2 * H), LZ)
        total = lap[f, pl.ds(8 * g, 8)] + dot(myb[...], block).reshape(8, LY, LZ)
        for r, weight in enumerate(COEFS, 1):
            total = total + weight * (fx[f, pl.ds(8 * g + 3 + r, 8)] - fx[f, pl.ds(8 * g + 4 - r, 8)])
        return total

    def source_field(g, _):
        rows = pl.ds(8 * g, 8)
        change = laplacian(0, g)
        lap[0, rows] = change
        value = change * u[1, pl.ds(H + 8 * g, 8), H : H + LY, :]
        for half in range(2):
            tmp[half, pl.ds(pl.multiple_of(g * 128, 128), 128), :] = value[:, :, half * 128 : half * 128 + 128].reshape(128, 128)
        tiles = []
        for y in range(LY):
            tiles.append([tmp[half, pl.ds(g * 128 + y, 8, stride=16), :] for half in range(2)])
        tiles = swap_groups(tiles)
        for m in range(BLOCKS):
            for half in range(2):
                con[m, pl.ds(pl.multiple_of(8 * g, 8), 8), half * 128 : half * 128 + 128] = tiles[m][half]
        return 0

    xg = {}

    lax.fori_loop(0, 4, source_field, 0)

    def send_back(*slots_of):
        n, start = len(slots_of), place[slots_of[0]]
        for e in range(1, NX):
            for d in slots_of:
                owner = lax.rem(gy + NY - d, NY) * NX + lax.rem(gx + e, NX)
                gst[e - 1, place[d]] = con[tbl_s[1, my_col, owner]]
            c = remote(
                gst.at[e - 1, pl.ds(start, n)], grecv.at[e - 1, pl.ds(start, n)],
                xg_s.at[e - 1, start], xg_r.at[e - 1, start], along_x(e),
            )
            c.start()
            xg[e, slots_of[0]] = c

    for group in ((4,), (3, 5), (2, 6), (1, 7), (0,)):
        send_back(*group)

    def scaled(g):
        v = vel[pl.ds(8 * g, 8)]
        return COURANT2 * (rho[pl.ds(H + 8 * g, 8), H : H + LY, :] * v * v)

    def update_source(g, _):
        rows = pl.ds(8 * g, 8)
        change = scaled(g) * lap[0, rows] - jnp.where(flat + g * (8 * NPY * LY * LZ) == cell_s, amp, 0.0)
        nx[0, rows] = nx[0, rows] + change
        return 0

    def update_adjoint(g, _):
        rows = pl.ds(8 * g, 8)
        nx[1, rows] = nx[1, rows] + scaled(g) * laplacian(1, g)
        return 0

    def sources_of(w):
        row = lax.broadcasted_iota(jnp.int32, (LX, 128), 0)
        lane = lax.broadcasted_iota(jnp.int32, (LX, 128), 1)
        cells = ((shot * HELD + w) * LX + row) * LZ + lane

        def body(r, totals):
            at = notes[r // NX, lax.rem(r, NX), 0:1, :].astype(jnp.int32)
            value = notes[r // NX, lax.rem(r, NX), 1:2, :]
            return tuple(
                total + jnp.where(cells + half * 128 == at, value, 0.0) for half, total in enumerate(totals)
            )

        zero = jnp.zeros((LX, 128), jnp.float32)
        totals = lax.fori_loop(0, NX * NY, body, (zero, zero))
        for half in range(2):
            spike[w, :, half * 128 : half * 128 + 128] = totals[half]

    def collect(*slots_of):
        for e in range(1, NX):
            xg[e, slots_of[0]].wait_recv()
        for d in slots_of:
            values = [con[tbl_s[1, my_col, owner_at(d)]]] + [grecv[NX - j - 1, place[d]] for j in range(1, NX)]
            picks = [within_of(j, d) for j in range(NX)]
            for w in range(HELD):
                total = None
                for j in range(NX):
                    term = jnp.where(picks[j] == w + 1, values[j], 0.0)
                    total = term if total is None else total + term
                part[d][w] = total

    ring = {}
    for d, to, target in ((4, 3, down), (3, 2, down), (2, 1, down), (1, 0, down), (4, 5, up), (5, 6, up), (6, 7, up), (7, 8, up)):
        for w in range(2):
            if d == 4 and w != (0 if to == 3 else 1):
                continue
            ring[to, w] = remote(
                part[d].at[halves[w]], rs.at[to, halves[w]], rs_s.at[to, w], rs_r.at[to, w], target
            )

    def add(d, w):
        ring[d, w].wait_recv()
        rows = slice(2 * w, 2 * w + 2)
        part[d][rows] = part[d][rows] + rs[d, rows]

    for d in (4, 5):
        note_y[d].wait_recv()
    for w in range(2):
        sources_of(w)
    depth_parts(1)
    collect(4)
    ring[3, 0].start()
    ring[5, 1].start()
    collect(3, 5)
    ring[2, 1].start()
    ring[6, 0].start()
    for w in range(2, HELD):
        sources_of(w)
    add(3, 0)
    ring[2, 0].start()
    add(5, 1)
    ring[6, 1].start()
    collect(2, 6)
    add(2, 1)
    ring[1, 1].start()
    add(6, 0)
    ring[7, 0].start()
    add(2, 0)
    ring[1, 0].start()
    add(6, 1)
    ring[7, 1].start()
    to_pencil(1, store_vel)
    collect(1, 7)
    add(1, 1)
    ring[0, 1].start()
    add(7, 0)
    ring[8, 0].start()
    add(1, 0)
    ring[0, 0].start()
    add(7, 1)
    ring[8, 1].start()
    collect(0)
    loads[4].wait()

    def settle(w, _):
        own_vel = chunk[1][0][w]
        gin[w] = gin[w] - (2.0 / own_vel) * spike[w]
        spike[w] = (2.0 * COURANT2) * (chunk[0][0][w] * own_vel)
        return 0

    lax.fori_loop(0, HELD, settle, 0)
    lax.fori_loop(0, 4, update_source, 0)
    out_f = pltpu.make_async_copy(nx.at[0], fwd_out, out_sem.at[0])
    out_f.start()
    wait_sides(halos[1])
    forward_xy(1)
    flux_x(1)
    flux_y(1)
    lax.fori_loop(0, 4, update_adjoint, 0)
    out_a = pltpu.make_async_copy(nx.at[1], adj_out, out_sem.at[1])
    out_a.start()
    for w in (1, 0):
        ring[0, w].wait_recv()
        ring[8, 1 - w].wait_recv()
    for w in range(HELD):
        gin[w] = gin[w] + spike[w] * (part[0][w] + (rs[0, w] + rs[8, w]))
    out_g = pltpu.make_async_copy(gin, grad_out, out_sem.at[2])
    out_g.start()

    for c in col_copies + note_x + list(note_y.values()) + sent[0] + sent[1] + list(xg.values()) + list(ring.values()):
        c.wait_send()
    for copies in ag:
        for c in copies.values():
            c.wait_send()
    finish_sides(halos[0])
    finish_sides(halos[1])
    finish_sides(rho_halo)
    out_f.wait()
    out_a.wait()
    out_g.wait()


def shards(
    fwd_now,
    fwd_next,
    adj_now,
    adj_next,
    velocity,
    density,
    gradient_in,
    block_home,
    aperture_col,
    source_cell,
    source_amp,
    receiver_cell,
    receiver_residual,
):
    f32, i32 = jnp.float32, jnp.int32
    any_space = pl.BlockSpec(memory_space=pl.ANY)
    pencil = (LX, LY, LZ)
    blocks = (HELD, LX, LZ)
    V = pltpu.VMEM
    D = pltpu.SemaphoreType.DMA
    scratch = [
        V((2, LX + 2 * H, LY + 2 * H, LZ), f32),
        V((2,) + pencil, f32),
        V((2, LX + 8, LY, LZ), f32),
        V((2, LX, LY + 2 * H, LZ), f32),
        V((2,) + pencil, f32),
        V((2,) + pencil, f32),
        V((LX + 2 * H, LY + 2 * H, LZ), f32),
        V(pencil, f32),
    ]
    scratch += [
        V((2, NX - 1, NY, LX, LZ), f32),
        V((NX * NY, LX, LZ), f32),
        V((NX * NY, LX, LZ), f32),
        V((2, LX * LY, 128), f32),
        V((2, 16, 8, LZ), f32),
        V((2, 16, 8, LZ), f32),
        V((BLOCKS, LX, LZ), f32),
        V((NX - 1, NY, LX, LZ), f32),
        V((NX - 1, NY, LX, LZ), f32),
        V(blocks, f32),
        V((9,) + blocks, f32),
        V((256, 256), f32),
        V((256, 256), f32),
        V((256, 256), f32),
        V((128, 256), f32),
        V((2, 8, 128), i32),
        pltpu.SMEM((2, 8, 128), i32),
        V((8, 128), i32),
        V((NX - 1, 8, 128), i32),
        pltpu.SMEM((NX - 1, 8, 128), i32),
        D((11,)),
        D((2, 8, 2)), D((2, 8, 2)),
        D((2, 3, 8)), D((2, 3, 8)),
        D((3, 8)), D((3, 8)),
        D((9, 2)), D((9, 2)),
        D((2, 4)), D((2, 4)),
        D((4,)), D((4,)),
        D((3,)), D((3,)),
        D((3,)),
        V((8, 16), i32),
        pltpu.SMEM((8, 16), i32),
        pltpu.SMEM((1,), i32),
        pltpu.SMEM((1,), i32),
        pltpu.SMEM((1,), f32),
        V((1, 256), i32),
        V((1, 256), f32),
        D((7,)),
        V((8, 128), f32),
        V((NY, NX, 8, 128), f32),
        V(blocks, f32),
        D((3,)), D((3,)),
        D((8,)), D((8,)),
    ]
    scratch += [V(blocks, f32) for _ in range(24)]
    fwd, adj, grad = pl.pallas_call(
        kernel,
        out_shape=(
            jax.ShapeDtypeStruct(pencil, f32),
            jax.ShapeDtypeStruct(pencil, f32),
            jax.ShapeDtypeStruct(blocks, f32),
        ),
        in_specs=[any_space] * 13,
        out_specs=(any_space, any_space, any_space),
        scratch_shapes=scratch,
        compiler_params=pltpu.CompilerParams(
            collective_id=0, has_side_effects=True, vmem_limit_bytes=62 * 2**20
        ),
        name="wave_step",
    )(
        fwd_now[0], adj_now[0], fwd_next[0], adj_next[0], velocity, density, gradient_in,
        block_home, aperture_col, source_cell, source_amp, receiver_cell, receiver_residual,
    )
    def settle_results(*refs):
        held, ins, outs = refs[6:9], refs[9], refs[10]
        coming, going = [], []
        for i in range(3):
            src, buf, dst = refs[i], held[i], refs[3 + i]
            pieces = 4 if i < 2 else 2
            rows = buf.shape[0] // pieces
            for k in range(pieces):
                at, n = pl.ds(k * rows, rows), len(coming)
                coming.append(pltpu.make_async_copy(src.at[at], buf.at[at], ins.at[n]))
                going.append(pltpu.make_async_copy(buf.at[at], dst.at[at], outs.at[n]))
        for c in coming:
            c.start()
        for c, g in zip(coming, going):
            c.wait()
            g.start()
        for g in going:
            g.wait()

    fwd, adj, grad = pl.pallas_call(
        settle_results,
        out_shape=(
            jax.ShapeDtypeStruct(pencil, f32),
            jax.ShapeDtypeStruct(pencil, f32),
            jax.ShapeDtypeStruct(blocks, f32),
        ),
        in_specs=[any_space] * 3,
        out_specs=(any_space, any_space, any_space),
        scratch_shapes=[V(pencil, f32), V(pencil, f32), V(blocks, f32), D((10,)), D((10,))],
        compiler_params=pltpu.CompilerParams(vmem_limit_bytes=62 * 2**20),
        name="results",
    )(fwd, adj, grad)
    return fwd[None], adj[None], grad


def solution(mesh):
    in_specs = (
        P("shot", "px", "py", None),
        P("shot", "px", "py", None),
        P("shot", "px", "py", None),
        P("shot", "px", "py", None),
        P("shot", "px", "py"),
        P("shot", "px", "py"),
        P("shot", "px", "py"),
        P(),
        P("shot"),
        P("shot"),
        P("shot"),
        P("shot", None),
        P("shot", None),
    )
    out_specs = (P("shot", "px", "py", None), P("shot", "px", "py", None), P("shot", "px", "py"))
    return jax.shard_map(shards, mesh=mesh, in_specs=in_specs, out_specs=out_specs, check_vma=False)
```

```python
import functools

import jax
import jax.numpy as jnp
from jax import lax
from jax.experimental import pallas as pl
from jax.experimental.pallas import tpu as pltpu
from jax.sharding import PartitionSpec as P

COEFS = (1225.0 / 1024.0, -245.0 / 3072.0, 49.0 / 5120.0, -5.0 / 7168.0)
COURANT2 = 0.01
MESH = pl.DeviceIdType.MESH
HIGHEST = lax.Precision.HIGHEST

LX, LY, LZ = 32, 16, 256
NY, NX = 8, 4
NPX, NPY = 4, 4
BLOCKS, HELD, BZ = 16, 4, 16
H = 8


def dot(a, b):
    return jnp.dot(a, b, precision=HIGHEST, preferred_element_type=jnp.float32)


def band(delta, pairs):
    total = jnp.zeros(delta.shape, jnp.float32)
    for offset, weight in pairs:
        total = jnp.where(delta == offset, jnp.float32(weight), total)
    return total


FORWARD = tuple((r, c) for r, c in enumerate(COEFS, 1)) + tuple((1 - r, -c) for r, c in enumerate(COEFS, 1))
BACKWARD = tuple((r - 1, c) for r, c in enumerate(COEFS, 1)) + tuple((-r, -c) for r, c in enumerate(COEFS, 1))


def swap_groups(tiles):
    lane = lax.broadcasted_iota(jnp.int32, (8, 128), 1)
    tiles = [list(t) for t in tiles]
    for a in range(8):
        tiles[a][1], tiles[a + 8][0] = tiles[a + 8][0], tiles[a][1]
    for k in (4, 2, 1):
        set_bit = ((lane >> 4) & k) != 0
        for a in range(16):
            if a & k:
                continue
            for half in range(2):
                low, high = tiles[a][half], tiles[a + k][half]
                tiles[a][half] = jnp.where(set_bit, pltpu.roll(high, 16 * k, 1), low)
                tiles[a + k][half] = jnp.where(set_bit, high, pltpu.roll(low, 128 - 16 * k, 1))
    return tiles


def kernel(
    fwd_now, adj_now, fwd_next, adj_next, velocity, density, gradient_in,
    home, col, source, amplitude, receivers, residuals,
    fwd_out, adj_out, grad_out,
    u, nx, fx, fy, fz, lap, rho, vel,
    std, got0, got1, tmp, sy, hy,
    con, gst, grecv, gin, rs,
    dz, dzb, my, myb,
    tbl_v, tbl_s, colbuf, colrecv, cols_s,
    loc_sem, ag_s, ag_r, xd_s, xd_r, xg_s, xg_r,
    rs_s, rs_r, uh_s, uh_r, dh_s, dh_r, col_ss, col_rs, out_sem,
    home_v, home_s, col_s, src_cell, src_amp, rec_cell, rec_val, small_sem,
    note, notes, spike, nx_s, nx_r, ny_s, ny_r,
    *slots,
):
    chunk = [slots[8 * c : 8 * c + 8] for c in range(2)]
    part = slots[16:24]
    got = (got0, got1)
    place = {0: 0, 1: 1, 7: 2, 2: 3, 6: 4, 3: 5, 5: 6, 4: 7}
    shot = lax.axis_index("shot")
    px = lax.axis_index("px")
    py = lax.axis_index("py")
    gx = lax.rem(shot, NX)
    gy = shot // NX

    def along_x(e):
        return {"shot": gy * NX + lax.rem(gx + e, NX)}

    def along_y(e):
        return {"shot": lax.rem(gy + e, NY) * NX + gx}

    own = (density, velocity)
    own_loads = [pltpu.make_async_copy(own[c], chunk[c][0], loc_sem.at[c]) for c in range(2)]
    loads = [
        pltpu.make_async_copy(fwd_now, u.at[0, pl.ds(H, LX), pl.ds(H, LY), :], loc_sem.at[4]),
        pltpu.make_async_copy(adj_now, u.at[1, pl.ds(H, LX), pl.ds(H, LY), :], loc_sem.at[5]),
        pltpu.make_async_copy(fwd_next, nx.at[0], loc_sem.at[6]),
        pltpu.make_async_copy(adj_next, nx.at[1], loc_sem.at[7]),
        pltpu.make_async_copy(gradient_in, gin, loc_sem.at[8]),
    ]
    small = [
        pltpu.make_async_copy(src, dst, small_sem.at[i])
        for i, (src, dst) in enumerate(
            (
                (col, col_s), (home, home_v), (home, home_s), (source, src_cell),
                (amplitude, src_amp), (receivers, rec_cell), (residuals, rec_val),
            )
        )
    ]
    for c in small + own_loads + loads:
        c.start()

    def zero_rows(start):
        def body(i, _):
            u[0, H + i, start : start + H, :] = jnp.zeros((H, LZ), jnp.float32)
            u[1, H + i, start : start + H, :] = jnp.zeros((H, LZ), jnp.float32)
            return 0

        lax.fori_loop(0, LX, body, 0)

    def zero_slabs(start):
        def body(i, _):
            u[0, start + i, H : H + LY, :] = jnp.zeros((LY, LZ), jnp.float32)
            u[1, start + i, H : H + LY, :] = jnp.zeros((LY, LZ), jnp.float32)
            return 0

        lax.fori_loop(0, H, body, 0)

    barrier = pltpu.get_barrier_semaphore()
    for target in [along_y(1), along_y(NY - 1)] + [along_x(e) for e in range(1, NX)]:
        pl.semaphore_signal(barrier, inc=1, device_id=target, device_id_type=MESH)
    sides = {
        "px_up": (px < NPX - 1, px > 0, {"px": px + 1}),
        "px_down": (px > 0, px < NPX - 1, {"px": px - 1}),
        "py_up": (py < NPY - 1, py > 0, {"py": py + 1}),
        "py_down": (py > 0, py < NPY - 1, {"py": py - 1}),
    }
    for has, _, target in sides.values():

        @pl.when(has)
        def _():
            pl.semaphore_signal(barrier, inc=1, device_id=target, device_id_type=MESH)

    small[0].wait()
    my_col = col_s[0]
    colbuf[...] = jnp.zeros((8, 128), jnp.int32) + my_col

    present = [jnp.where(has, 1, 0) for has, _, _ in sides.values()]
    pl.semaphore_wait(barrier, NX + 1 + sum(present))

    def remote(src, dst, ss, rr, target):
        return pltpu.make_async_remote_copy(
            src_ref=src, dst_ref=dst, send_sem=ss, recv_sem=rr, device_id=target, device_id_type=MESH
        )

    col_copies = [
        remote(colbuf, colrecv.at[e - 1], col_ss.at[e - 1], col_rs.at[e - 1], along_x(e)) for e in range(1, NX)
    ]
    for c in col_copies:
        c.start()

    up, down = along_y(1), along_y(NY - 1)

    halves = (pl.ds(0, 2), pl.ds(2, 2))

    def gather(c):
        b, out = chunk[c], {}
        for d, src, target in (
            (1, own[c], up), (7, own[c], down), (2, b[1], up), (6, b[7], down),
            (3, b[2], up), (5, b[6], down), (4, b[3], up), (4, b[5], down),
        ):
            for w in range(2):
                if d == 4 and w != (0 if target is up else 1):
                    continue
                out[d, w] = remote(src.at[halves[w]], b[d].at[halves[w]], ag_s.at[c, d, w], ag_r.at[c, d, w], target)
        return out

    ag = [gather(c) for c in range(2)]

    def first(c):
        for w in range(2):
            ag[c][1, w].start()
            ag[c][7, w].start()

    def forward(c, d):
        for w in range(2):
            for k, to in ((d, d + 1), (NY - d, NY - d - 1)):
                ag[c][k, w].wait_recv()
                if (to, w) in ag[c] and not (to == 4 and w != (0 if k == 3 else 1)):
                    ag[c][to, w].start()

    first(0)

    def halo(f, field):
        s, r = uh_s, uh_r
        return {
            "py_up": remote(field.at[:, pl.ds(LY - H, H), :], u.at[f, pl.ds(H, LX), pl.ds(0, H), :], s.at[f, 0], r.at[f, 0], sides["py_up"][2]),
            "py_down": remote(field.at[:, pl.ds(0, H), :], u.at[f, pl.ds(H, LX), pl.ds(H + LY, H), :], s.at[f, 1], r.at[f, 1], sides["py_down"][2]),
            "px_up": remote(field.at[pl.ds(LX - H, H)], u.at[f, pl.ds(0, H), pl.ds(H, LY), :], s.at[f, 2], r.at[f, 2], sides["px_up"][2]),
            "px_down": remote(field.at[pl.ds(0, H)], u.at[f, pl.ds(H + LX, H), pl.ds(H, LY), :], s.at[f, 3], r.at[f, 3], sides["px_down"][2]),
        }

    def start_sides(copies):
        for name, c in copies.items():
            pl.when(sides[name][0])(c.start)

    def wait_sides(copies):
        for name, c in copies.items():
            pl.when(sides[name][1])(c.wait_recv)

    def finish_sides(copies):
        for name, c in copies.items():
            pl.when(sides[name][0])(c.wait_send)

    halos = [halo(0, fwd_now), halo(1, adj_now)]
    start_sides(halos[0])
    small[1].wait()
    small[2].wait()
    lane8 = lax.broadcasted_iota(jnp.int32, (8, 128), 1)
    within = jnp.zeros((8, 128), jnp.int32)
    depth_of = jnp.zeros((8, 128), jnp.int32)
    for m in range(BLOCKS):
        h = home_v[:, m : m + 1]
        hit = (h >> 2) == lane8
        within = jnp.where(hit, (h & 3) + 1, within)
        depth_of = jnp.where(hit, m, depth_of)
    tbl_v[0] = within
    tbl_v[1] = depth_of
    table_copy = pltpu.make_async_copy(tbl_v, tbl_s, loc_sem.at[9])
    table_copy.start()
    pl.when(py == 0)(lambda: zero_rows(0))
    pl.when(py == NPY - 1)(lambda: zero_rows(H + LY))
    pl.when(px == 0)(lambda: zero_slabs(0))
    pl.when(px == NPX - 1)(lambda: zero_slabs(H + LX))

    for c in col_copies:
        c.wait_recv()
    cols_copy = pltpu.make_async_copy(colrecv, cols_s, loc_sem.at[10])
    cols_copy.start()
    table_copy.wait()
    cols_copy.wait()
    cols = [my_col] + [cols_s[NX - j - 1, 0, 0] for j in range(1, NX)]

    def owner_at(d):
        return lax.rem(gy + NY - d, NY) * NX + gx

    def within_of(j, d):
        return tbl_s[0, cols[j], owner_at(d)]

    sent = [[], []]

    def serve(c, *slots_of):
        n, start = len(slots_of), place[slots_of[0]]
        for e in range(1, NX):
            for d in slots_of:
                std[c, e - 1, place[d]] = chunk[c][d][jnp.maximum(within_of(e, d) - 1, 0)]
            x = remote(
                std.at[c, e - 1, pl.ds(start, n)], got[c].at[pl.ds(e * NY + start, n)],
                xd_s.at[c, e - 1, start], xd_r.at[c, e - 1, start], along_x(e),
            )
            x.start()
            sent[c].append(x)
        for d in slots_of:
            got[c][place[d]] = chunk[c][d][jnp.maximum(within_of(0, d) - 1, 0)]

    def step(c, d):
        forward(c, d)
        serve(c, d, NY - d)

    def last(c):
        ag[c][4, 0].wait_recv()
        ag[c][4, 1].wait_recv()
        serve(c, 4)

    def place_of(m):
        owner = home_s[my_col, m] >> 2
        d = (gy - (owner >> 2)) & 7
        at = jnp.where(d == 0, 0, jnp.where(d <= 4, 2 * d - 1, 16 - 2 * d))
        return ((gx - (owner & 3)) & 3) * NY + at

    own_loads[0].wait()
    serve(0, 0)

    def build(i, _):
        start = pl.multiple_of(i * 32, 32)
        row = lax.broadcasted_iota(jnp.int32, (32, 256), 0) + start
        colm = lax.broadcasted_iota(jnp.int32, (32, 256), 1)
        forward = jnp.where(colm < LZ - 1, band(row - colm, FORWARD), 0.0)
        dz[pl.ds(start, 32), :] = forward
        dzb[pl.ds(start, 32), :] = band(row - colm, BACKWARD)
        same = (row >> 5) == (colm >> 5)
        my[pl.ds(start, 32), :] = jnp.where(same, band(colm - row, FORWARD), 0.0)
        return 0

    lax.fori_loop(0, 8, build, 0)

    def build_back(i, _):
        start = pl.multiple_of(i * 32, 32)
        row = lax.broadcasted_iota(jnp.int32, (32, 256), 0) + start
        colm = lax.broadcasted_iota(jnp.int32, (32, 256), 1)
        same = (row >> 4) == (colm >> 5)
        delta = ((colm & 31) - H) - (row & 15)
        myb[pl.ds(start, 32), :] = jnp.where(same, band(delta, BACKWARD), 0.0)
        return 0

    lax.fori_loop(0, 4, build_back, 0)

    step(0, 1)

    loads[0].wait()
    loads[1].wait()

    def forward_z(f):
        def body(g, _):
            block = u[f, pl.ds(H + 8 * g, 8), H : H + LY, :].reshape(8 * LY, LZ)
            fz[f, pl.ds(8 * g, 8)] = dot(block, dz[...]).reshape(8, LY, LZ)
            return 0

        lax.fori_loop(0, 4, body, 0)

    for c in small[3:]:
        c.wait()
    cell_s = src_cell[0]
    amp = src_amp[0]
    shape = (8, LY, LZ)
    iota_x = lax.broadcasted_iota(jnp.int32, shape, 0)
    iota_y = lax.broadcasted_iota(jnp.int32, shape, 1)
    iota_z = lax.broadcasted_iota(jnp.int32, shape, 2)
    flat = ((iota_x + px * LX) * (NPY * LY) + iota_y + py * LY) * LZ + iota_z
    note_x = [
        remote(note, notes.at[0, e], nx_s.at[e - 1], nx_r.at[e - 1], along_x(e)) for e in range(1, NX)
    ]
    note_y = {}
    for d, k, target in ((1, 0, up), (2, 1, up), (3, 2, up), (4, 3, up), (7, 0, down), (6, 7, down), (5, 6, down)):
        note_y[d] = remote(notes.at[k], notes.at[d], ny_s.at[d], ny_r.at[d], target)

    def write_note():
        def body(g, total):
            block = u[1, pl.ds(H + 8 * g, 8), H : H + LY, :]
            hit = jnp.where(flat + g * (8 * NPY * LY * LZ) == cell_s, block, 0.0)
            return total + jnp.sum(hit, axis=0)

        value = jnp.sum(lax.fori_loop(0, 4, body, jnp.zeros((LY, LZ), jnp.float32))) * amp
        x, y, z = (cell_s >> 14) - px * LX, ((cell_s >> 8) & 63) - py * LY, cell_s & 255
        mine = (x >= 0) & (x < LX) & (y >= 0) & (y < LY)
        block = home_s[my_col, z >> 4]
        at = jnp.where(mine, block * (LX * LZ) + x * LZ + y * BZ + (z & 15), -1)
        row = lax.broadcasted_iota(jnp.int32, (8, 128), 0)
        tile = jnp.where(row == 0, at.astype(jnp.float32), value)
        note[...] = tile
        notes[0, 0] = tile
        for c in note_x:
            c.start()

    forward_z(0)
    step(0, 2)
    first(1)
    write_note()
    step(0, 3)
    for c in note_x:
        c.wait_recv()
    note_y[1].start()
    note_y[7].start()
    forward_z(1)

    cell = rec_cell[...]
    cell_x = (cell >> 14) - px * LX
    cell_y = ((cell >> 8) & 63) - py * LY
    cell_z = cell & 255
    here = (cell_x >= 0) & (cell_x < LX) & (cell_y >= 0) & (cell_y < LY)
    spot = jnp.where(here, cell_x * LY + cell_y, -1)
    by_depth = jnp.where(lax.broadcasted_iota(jnp.int32, (LZ, 256), 0) == cell_z, rec_val[...], 0.0)
    loads[2].wait()
    loads[3].wait()

    def bases(g, _):
        start = pl.multiple_of(g * 128, 128)
        at = (lax.broadcasted_iota(jnp.int32, (128, 256), 0) + start == spot).astype(jnp.float32)
        added = lax.dot_general(
            at, by_depth, (((1,), (1,)), ((), ())), precision=HIGHEST, preferred_element_type=jnp.float32
        ).reshape(8, LY, LZ)
        rows = pl.ds(8 * g, 8)
        nx[0, rows] = 2.0 * u[0, pl.ds(H + 8 * g, 8), H : H + LY, :] - nx[0, rows]
        nx[1, rows] = 2.0 * u[1, pl.ds(H + 8 * g, 8), H : H + LY, :] - nx[1, rows] + added
        return 0

    lax.fori_loop(0, 4, bases, 0)

    last(0)
    own_loads[1].wait()
    serve(1, 0)

    def forward_xy(f):
        def body_x(k, _):
            total = None
            for r, weight in enumerate(COEFS, 1):
                term = weight * (u[f, k + 4 + r, H : H + LY, :] - u[f, k + 5 - r, H : H + LY, :])
                total = term if total is None else total + term
            fx[f, k] = total
            return 0

        lax.fori_loop(0, LX + 7, body_x, 0)

        def body_y(g, _):
            block = u[f, pl.ds(H + 8 * g, 8)].reshape(8 * (LY + 2 * H), LZ)
            fy[f, pl.ds(8 * g, 8)] = dot(my[...], block).reshape(8, LY + 2 * H, LZ)
            return 0

        lax.fori_loop(0, 4, body_y, 0)

    wait_sides(halos[0])
    forward_xy(0)
    step(1, 1)

    def to_pencil(c, store):
        for x in sent[c]:
            x.wait_recv()
        places = [place_of(m) for m in range(BLOCKS)]

        def body(k, _):
            tiles = []
            for m in range(BLOCKS):
                slab = got[c][places[m], pl.ds(pl.multiple_of(8 * k, 8), 8), :]
                tiles.append([slab[:, :128], slab[:, 128:]])
            tiles = swap_groups(tiles)
            for y in range(LY):
                for half in range(2):
                    tmp[half, pl.ds(k * 128 + y, 8, stride=16), :] = tiles[y][half]
            for half in range(2):
                rows = tmp[half, pl.ds(pl.multiple_of(k * 128, 128), 128), :]
                store(k, half, rows.reshape(8, LY, 128))
            return 0

        lax.fori_loop(0, 4, body, 0)

    def store_rho(g, half, value):
        rho[pl.ds(H + 8 * g, 8), H : H + LY, half * 128 : half * 128 + 128] = value

    def store_vel(g, half, value):
        vel[pl.ds(8 * g, 8), :, half * 128 : half * 128 + 128] = value

    to_pencil(0, store_rho)

    def pack(i, _):
        sy[0, i, 0:4, :] = rho[H + i, H + 12 : H + 16, :]
        sy[0, i, 4:8, :] = rho[H + 16 + i, H + 12 : H + 16, :]
        sy[1, i, 0:4, :] = rho[H + i, H : H + 4, :]
        sy[1, i, 4:8, :] = rho[H + 16 + i, H : H + 4, :]
        return 0

    lax.fori_loop(0, 16, pack, 0)
    rho_halo = {
        "py_up": remote(sy.at[0], hy.at[0], dh_s.at[0], dh_r.at[0], sides["py_up"][2]),
        "py_down": remote(sy.at[1], hy.at[1], dh_s.at[1], dh_r.at[1], sides["py_down"][2]),
        "px_up": remote(rho.at[pl.ds(H + LX - 4, 4), pl.ds(H, LY), :], rho.at[pl.ds(H - 4, 4), pl.ds(H, LY), :], dh_s.at[2], dh_r.at[2], sides["px_up"][2]),
        "px_down": remote(rho.at[pl.ds(H, 4), pl.ds(H, LY), :], rho.at[pl.ds(H + LX, 4), pl.ds(H, LY), :], dh_s.at[3], dh_r.at[3], sides["px_down"][2]),
    }
    start_sides(rho_halo)
    step(1, 2)
    for d, k in ((1, 2), (7, 6)):
        note_y[d].wait_recv()
        note_y[k].start()

    def depth_part(f, g):
        block = rho[pl.ds(H + 8 * g, 8), H : H + LY, :].reshape(8 * LY, LZ)
        scale = 2.0 / (block + pltpu.roll(block, LZ - 1, 1))
        rows = pl.ds(8 * g, 8)
        flux = fz[f, rows].reshape(8 * LY, LZ) * scale
        lap[f, rows] = dot(flux, dzb[...]).reshape(8, LY, LZ)

    def depth_parts(f):
        def body(g, _):
            depth_part(f, g)
            return 0

        lax.fori_loop(0, 4, body, 0)

    depth_parts(0)
    step(1, 3)
    for d, k in ((2, 3), (6, 5)):
        note_y[d].wait_recv()
        note_y[k].start()

    note_y[3].wait_recv()
    note_y[4].start()
    last(1)

    wait_sides(rho_halo)
    start_sides(halos[1])

    @pl.when(py > 0)
    def _():
        def body(i, _):
            rho[H + i, H - 4 : H, :] = hy[0, i, 0:4, :]
            rho[H + 16 + i, H - 4 : H, :] = hy[0, i, 4:8, :]
            return 0

        lax.fori_loop(0, 16, body, 0)

    @pl.when(py < NPY - 1)
    def _():
        def body(i, _):
            rho[H + i, H + LY : H + LY + 4, :] = hy[1, i, 0:4, :]
            rho[H + 16 + i, H + LY : H + LY + 4, :] = hy[1, i, 4:8, :]
            return 0

        lax.fori_loop(0, 16, body, 0)

    def flux_x(f):
        def body(k, _):
            face = px * LX + k - 4
            open_x = (face >= 0) & (face <= NPX * LX - 2)
            scale = jnp.where(open_x, 2.0 / (rho[k + 4, H : H + LY, :] + rho[k + 5, H : H + LY, :]), 0.0)
            fx[f, k] = fx[f, k] * scale
            return 0

        lax.fori_loop(0, LX + 7, body, 0)

    rows_y = lax.broadcasted_iota(jnp.int32, (LY + 2 * H, LZ), 0) - H
    face_y = rows_y + py * LY
    open_y = (rows_y >= -4) & (rows_y < LY + 3) & (face_y >= 0) & (face_y <= NPY * LY - 2)

    def flux_y(f):
        def body(i, _):
            line = rho[H + i]
            scale = jnp.where(open_y, 2.0 / (line + pltpu.roll(line, LY + 2 * H - 1, 0)), 0.0)
            fy[f, i] = fy[f, i] * scale
            return 0

        lax.fori_loop(0, LX, body, 0)

    flux_x(0)
    flux_y(0)

    def laplacian(f, g):
        block = fy[f, pl.ds(8 * g, 8)].reshape(8 * (LY + 2 * H), LZ)
        total = lap[f, pl.ds(8 * g, 8)] + dot(myb[...], block).reshape(8, LY, LZ)
        for r, weight in enumerate(COEFS, 1):
            total = total + weight * (fx[f, pl.ds(8 * g + 3 + r, 8)] - fx[f, pl.ds(8 * g + 4 - r, 8)])
        return total

    def source_field(g, _):
        rows = pl.ds(8 * g, 8)
        change = laplacian(0, g)
        lap[0, rows] = change
        value = change * u[1, pl.ds(H + 8 * g, 8), H : H + LY, :]
        for half in range(2):
            tmp[half, pl.ds(pl.multiple_of(g * 128, 128), 128), :] = value[:, :, half * 128 : half * 128 + 128].reshape(128, 128)
        tiles = []
        for y in range(LY):
            tiles.append([tmp[half, pl.ds(g * 128 + y, 8, stride=16), :] for half in range(2)])
        tiles = swap_groups(tiles)
        for m in range(BLOCKS):
            for half in range(2):
                con[m, pl.ds(pl.multiple_of(8 * g, 8), 8), half * 128 : half * 128 + 128] = tiles[m][half]
        return 0

    xg = {}

    lax.fori_loop(0, 4, source_field, 0)

    def send_back(*slots_of):
        n, start = len(slots_of), place[slots_of[0]]
        for e in range(1, NX):
            for d in slots_of:
                owner = lax.rem(gy + NY - d, NY) * NX + lax.rem(gx + e, NX)
                gst[e - 1, place[d]] = con[tbl_s[1, my_col, owner]]
            c = remote(
                gst.at[e - 1, pl.ds(start, n)], grecv.at[e - 1, pl.ds(start, n)],
                xg_s.at[e - 1, start], xg_r.at[e - 1, start], along_x(e),
            )
            c.start()
            xg[e, slots_of[0]] = c

    for group in ((4,), (3, 5), (2, 6), (1, 7), (0,)):
        send_back(*group)

    def scaled(g):
        v = vel[pl.ds(8 * g, 8)]
        return COURANT2 * (rho[pl.ds(H + 8 * g, 8), H : H + LY, :] * v * v)

    def update_source(g, _):
        rows = pl.ds(8 * g, 8)
        change = scaled(g) * lap[0, rows] - jnp.where(flat + g * (8 * NPY * LY * LZ) == cell_s, amp, 0.0)
        nx[0, rows] = nx[0, rows] + change
        return 0

    def update_adjoint(g, _):
        rows = pl.ds(8 * g, 8)
        nx[1, rows] = nx[1, rows] + scaled(g) * laplacian(1, g)
        return 0

    def sources_of(w):
        row = lax.broadcasted_iota(jnp.int32, (LX, 128), 0)
        lane = lax.broadcasted_iota(jnp.int32, (LX, 128), 1)
        cells = ((shot * HELD + w) * LX + row) * LZ + lane

        def body(r, totals):
            at = notes[r // NX, lax.rem(r, NX), 0:1, :].astype(jnp.int32)
            value = notes[r // NX, lax.rem(r, NX), 1:2, :]
            return tuple(
                total + jnp.where(cells + half * 128 == at, value, 0.0) for half, total in enumerate(totals)
            )

        zero = jnp.zeros((LX, 128), jnp.float32)
        totals = lax.fori_loop(0, NX * NY, body, (zero, zero))
        for half in range(2):
            spike[w, :, half * 128 : half * 128 + 128] = totals[half]

    def collect(*slots_of):
        for e in range(1, NX):
            xg[e, slots_of[0]].wait_recv()
        for d in slots_of:
            values = [con[tbl_s[1, my_col, owner_at(d)]]] + [grecv[NX - j - 1, place[d]] for j in range(1, NX)]
            picks = [within_of(j, d) for j in range(NX)]
            for w in range(HELD):
                total = None
                for j in range(NX):
                    term = jnp.where(picks[j] == w + 1, values[j], 0.0)
                    total = term if total is None else total + term
                part[d][w] = total

    ring = {}
    for d, to, target in ((4, 3, down), (3, 2, down), (2, 1, down), (1, 0, down), (4, 5, up), (5, 6, up), (6, 7, up), (7, 8, up)):
        for w in range(2):
            if d == 4 and w != (0 if to == 3 else 1):
                continue
            ring[to, w] = remote(
                part[d].at[halves[w]], rs.at[to, halves[w]], rs_s.at[to, w], rs_r.at[to, w], target
            )

    def add(d, w):
        ring[d, w].wait_recv()
        rows = slice(2 * w, 2 * w + 2)
        part[d][rows] = part[d][rows] + rs[d, rows]

    for d in (4, 5):
        note_y[d].wait_recv()
    for w in range(2):
        sources_of(w)
    depth_parts(1)
    collect(4)
    ring[3, 0].start()
    ring[5, 1].start()
    collect(3, 5)
    ring[2, 1].start()
    ring[6, 0].start()
    for w in range(2, HELD):
        sources_of(w)
    add(3, 0)
    ring[2, 0].start()
    add(5, 1)
    ring[6, 1].start()
    collect(2, 6)
    add(2, 1)
    ring[1, 1].start()
    add(6, 0)
    ring[7, 0].start()
    add(2, 0)
    ring[1, 0].start()
    add(6, 1)
    ring[7, 1].start()
    to_pencil(1, store_vel)
    collect(1, 7)
    add(1, 1)
    ring[0, 1].start()
    add(7, 0)
    ring[8, 0].start()
    add(1, 0)
    ring[0, 0].start()
    add(7, 1)
    ring[8, 1].start()
    collect(0)
    loads[4].wait()

    def settle(w, _):
        own_vel = chunk[1][0][w]
        gin[w] = gin[w] - (2.0 / own_vel) * spike[w]
        spike[w] = (2.0 * COURANT2) * (chunk[0][0][w] * own_vel)
        return 0

    lax.fori_loop(0, HELD, settle, 0)
    lax.fori_loop(0, 4, update_source, 0)
    out_f = pltpu.make_async_copy(nx.at[0], fwd_out, out_sem.at[0])
    out_f.start()
    wait_sides(halos[1])
    forward_xy(1)
    flux_x(1)
    flux_y(1)
    lax.fori_loop(0, 4, update_adjoint, 0)
    out_a = pltpu.make_async_copy(nx.at[1], adj_out, out_sem.at[1])
    out_a.start()
    for w in (1, 0):
        ring[0, w].wait_recv()
        ring[8, 1 - w].wait_recv()
    for w in range(HELD):
        gin[w] = gin[w] + spike[w] * (part[0][w] + (rs[0, w] + rs[8, w]))
    out_g = pltpu.make_async_copy(gin, grad_out, out_sem.at[2])
    out_g.start()

    for c in col_copies + note_x + list(note_y.values()) + sent[0] + sent[1] + list(xg.values()) + list(ring.values()):
        c.wait_send()
    for copies in ag:
        for c in copies.values():
            c.wait_send()
    finish_sides(halos[0])
    finish_sides(halos[1])
    finish_sides(rho_halo)
    out_f.wait()
    out_a.wait()
    out_g.wait()


def shards(
    fwd_now,
    fwd_next,
    adj_now,
    adj_next,
    velocity,
    density,
    gradient_in,
    block_home,
    aperture_col,
    source_cell,
    source_amp,
    receiver_cell,
    receiver_residual,
):
    f32, i32 = jnp.float32, jnp.int32
    any_space = pl.BlockSpec(memory_space=pl.ANY)
    pencil = (LX, LY, LZ)
    blocks = (HELD, LX, LZ)
    V = pltpu.VMEM
    D = pltpu.SemaphoreType.DMA
    scratch = [
        V((2, LX + 2 * H, LY + 2 * H, LZ), f32),
        V((2,) + pencil, f32),
        V((2, LX + 8, LY, LZ), f32),
        V((2, LX, LY + 2 * H, LZ), f32),
        V((2,) + pencil, f32),
        V((2,) + pencil, f32),
        V((LX + 2 * H, LY + 2 * H, LZ), f32),
        V(pencil, f32),
    ]
    scratch += [
        V((2, NX - 1, NY, LX, LZ), f32),
        V((NX * NY, LX, LZ), f32),
        V((NX * NY, LX, LZ), f32),
        V((2, LX * LY, 128), f32),
        V((2, 16, 8, LZ), f32),
        V((2, 16, 8, LZ), f32),
        V((BLOCKS, LX, LZ), f32),
        V((NX - 1, NY, LX, LZ), f32),
        V((NX - 1, NY, LX, LZ), f32),
        V(blocks, f32),
        V((9,) + blocks, f32),
        V((256, 256), f32),
        V((256, 256), f32),
        V((256, 256), f32),
        V((128, 256), f32),
        V((2, 8, 128), i32),
        pltpu.SMEM((2, 8, 128), i32),
        V((8, 128), i32),
        V((NX - 1, 8, 128), i32),
        pltpu.SMEM((NX - 1, 8, 128), i32),
        D((11,)),
        D((2, 8, 2)), D((2, 8, 2)),
        D((2, 3, 8)), D((2, 3, 8)),
        D((3, 8)), D((3, 8)),
        D((9, 2)), D((9, 2)),
        D((2, 4)), D((2, 4)),
        D((4,)), D((4,)),
        D((3,)), D((3,)),
        D((3,)),
        V((8, 16), i32),
        pltpu.SMEM((8, 16), i32),
        pltpu.SMEM((1,), i32),
        pltpu.SMEM((1,), i32),
        pltpu.SMEM((1,), f32),
        V((1, 256), i32),
        V((1, 256), f32),
        D((7,)),
        V((8, 128), f32),
        V((NY, NX, 8, 128), f32),
        V(blocks, f32),
        D((3,)), D((3,)),
        D((8,)), D((8,)),
    ]
    scratch += [V(blocks, f32) for _ in range(24)]
    fwd, adj, grad = pl.pallas_call(
        kernel,
        out_shape=(
            jax.ShapeDtypeStruct(pencil, f32),
            jax.ShapeDtypeStruct(pencil, f32),
            jax.ShapeDtypeStruct(blocks, f32),
        ),
        in_specs=[any_space] * 13,
        out_specs=(any_space, any_space, any_space),
        scratch_shapes=scratch,
        compiler_params=pltpu.CompilerParams(
            collective_id=0, has_side_effects=True, vmem_limit_bytes=62 * 2**20
        ),
        name="wave_step",
    )(
        fwd_now[0], adj_now[0], fwd_next[0], adj_next[0], velocity, density, gradient_in,
        block_home, aperture_col, source_cell, source_amp, receiver_cell, receiver_residual,
    )
    def settle_results(*refs):
        held, ins, outs = refs[6:9], refs[9], refs[10]
        coming, going = [], []
        for i in range(3):
            src, buf, dst = refs[i], held[i], refs[3 + i]
            pieces = 4 if i < 2 else 2
            rows = buf.shape[0] // pieces
            for k in range(pieces):
                at, n = pl.ds(k * rows, rows), len(coming)
                coming.append(pltpu.make_async_copy(src.at[at], buf.at[at], ins.at[n]))
                going.append(pltpu.make_async_copy(buf.at[at], dst.at[at], outs.at[n]))
        for c in coming:
            c.start()
        for c, g in zip(coming, going):
            c.wait()
            g.start()
        for g in going:
            g.wait()

    fwd, adj, grad = pl.pallas_call(
        settle_results,
        out_shape=(
            jax.ShapeDtypeStruct(pencil, f32),
            jax.ShapeDtypeStruct(pencil, f32),
            jax.ShapeDtypeStruct(blocks, f32),
        ),
        in_specs=[any_space] * 3,
        out_specs=(any_space, any_space, any_space),
        scratch_shapes=[V(pencil, f32), V(pencil, f32), V(blocks, f32), D((10,)), D((10,))],
        compiler_params=pltpu.CompilerParams(vmem_limit_bytes=62 * 2**20),
        name="results",
    )(fwd, adj, grad)
    return fwd[None], adj[None], grad


def solution(mesh):
    in_specs = (
        P("shot", "px", "py", None),
        P("shot", "px", "py", None),
        P("shot", "px", "py", None),
        P("shot", "px", "py", None),
        P("shot", "px", "py"),
        P("shot", "px", "py"),
        P("shot", "px", "py"),
        P(),
        P("shot"),
        P("shot"),
        P("shot"),
        P("shot", None),
        P("shot", None),
    )
    out_specs = (P("shot", "px", "py", None), P("shot", "px", "py", None), P("shot", "px", "py"))
    return jax.shard_map(shards, mesh=mesh, in_specs=in_specs, out_specs=out_specs, check_vma=False)
```
